256 devices in a mesh: tm: 16 (over y, x), space: 16 (over z, core).
Axes of the slice: x: 4, y: 4, z: 8, core: 2. Of those that a mesh axis runs over, the one named last changes fastest.
Arguments:
- starts: float32 [16, 3, 128, 64, 128], P('tm', None, 'space'), may hold values from -6 to 6
- strain: bfloat16 [16, 9, 128, 64, 128], P('tm', None, 'space'), may hold values from -0.59765625 to 0.59765625
Outputs:
- corrected: float32 [16, 3, 128, 64, 128], P('tm', None, 'space')
The draws below stay inside these ranges and needn't reach their ends.
All inputs are finite; a program needn't handle non-finite values.
Results may differ from the reference program's by a relative error of at most 0.0003.
Values sent between devices are 32-bit elements; how exact they have to be, the bound alone decides.
No kernel may reach another device: no remote copies, remote signals or barrier semaphores. Data moves between devices by JAX's collectives and lax.ppermute only.
A program may use at most 128 MiB of HBM per device.

```python
import jax
import jax.numpy as jnp
from jax import lax

CX = 64
CY = 128
COARSEN = 4
SLICES = 16
NZ = 128


def block_levels(own_key, dims, pieces, low, high):
    loudness, own = 1.0, jax.random.fold_in(own_key, 6)
    for dim, parts in pieces:
        steps = jnp.exp(jax.random.uniform(jax.random.fold_in(own, dim), (parts,), jnp.float32, low / len(pieces), high / len(pieces)))
        loudness = loudness * jnp.repeat(steps, dims[dim] // parts).reshape([-1 if axis == dim else 1 for axis in range(len(dims))])
    return loudness


def normal_values(stream_key, extent, scale, reach, pieces=(), dtype=jnp.bfloat16):
    values = jax.random.normal(stream_key, extent, jnp.float32) * scale
    if len(pieces) > 0:
        values = block_levels(stream_key, extent, pieces, -0.22, 0.18) * values
    return jnp.clip(values, min=-reach, max=reach).astype(dtype)


def setup_inputs(seed: int = 0) -> dict:
    streams_of = jax.random.split(jax.random.key(seed), 3)
    starts = normal_values(streams_of[0], (SLICES, 3, NZ, CX, CY), 1.0, 6.0, ((0, 16), (2, 16)), jnp.float32)
    strain = normal_values(streams_of[1], (SLICES, 9, NZ, CX, CY), 0.1, 0.59765625, ((0, 16), (2, 16)))
    return {"starts": starts, "strain": strain}


kernel_near = 0.8
kernel_far = 0.2
diffusion = 0.08
coarse_rate = 0.1

def depth_terms(padded, field, depth):
    near_sum = padded[:, 3:3 + depth] + padded[:, 1:1 + depth] - 2.0 * field
    far_sum = padded[:, 4:4 + depth] + padded[:, 0:depth] - 2.0 * field
    return kernel_near * near_sum + kernel_far * far_sum

def plane_terms(field):
    total = jnp.zeros_like(field)
    for along in (2, 3):
        near_sum = jnp.roll(field, 1, along) + jnp.roll(field, -1, along) - 2.0 * field
        far_sum = jnp.roll(field, 2, along) + jnp.roll(field, -2, along) - 2.0 * field
        total = total + kernel_near * near_sum + kernel_far * far_sum
    return total

def stretch_terms(field, strain):
    result = []
    for row in range(3):
        acc = strain[3 * row].astype(jnp.float32) * field[0]
        acc = acc + strain[3 * row + 1].astype(jnp.float32) * field[1]
        acc = acc + strain[3 * row + 2].astype(jnp.float32) * field[2]
        result.append(acc)
    return jnp.stack(result, axis=0)

def fine_step(field, strain):
    depth = field.shape[1]
    padded = jnp.pad(field, ((0, 0), (2, 2), (0, 0), (0, 0)))
    return field + stretch_terms(field, strain) + diffusion * (depth_terms(padded, field, depth) + plane_terms(field))

def restrict_field(field):
    comps, depth, width_x, width_y = field.shape
    blocks = field.reshape(comps, depth // COARSEN, COARSEN, width_x // COARSEN, COARSEN, width_y // COARSEN, COARSEN)
    return jnp.mean(blocks, axis=(2, 4, 6))

def prolong_field(coarse):
    comps, depth, width_x, width_y = coarse.shape
    spread = jnp.broadcast_to(coarse[:, :, None, :, None, :, None], (comps, depth, COARSEN, width_x, COARSEN, width_y, COARSEN))
    return spread.reshape(comps, depth * COARSEN, width_x * COARSEN, width_y * COARSEN)

def coarse_step(field, padded):
    near_sum = padded[..., 2:, :, :] + padded[..., :-2, :, :]
    near_sum = near_sum + jnp.roll(field, 1, -2) + jnp.roll(field, -1, -2)
    near_sum = near_sum + jnp.roll(field, 1, -1) + jnp.roll(field, -1, -1)
    return field + coarse_rate * (near_sum - 6.0 * field)

def solve_small(factor, vector):
    lower = lax.linalg.triangular_solve(factor, vector[:, None], left_side=True, lower=True)
    upper = lax.linalg.triangular_solve(factor, lower, left_side=True, lower=True, transpose_a=True)
    return upper[:, 0]

def reference(starts, strain):
    count = starts.shape[0]
    fine_ends = lax.map(lambda inputs: fine_step(inputs[0], inputs[1]), (starts, strain))
    snap_basis = jnp.stack([restrict_field(starts[index]) for index in range(count)], axis=0)
    images = jnp.stack([restrict_field(fine_ends[index]) for index in range(count)], axis=0)
    flat_basis = snap_basis.reshape(count, -1)
    flat_images = images.reshape(count, -1)
    gram_matrix = jnp.dot(flat_basis, flat_basis.T, precision=lax.Precision.HIGHEST)
    factor = jnp.linalg.cholesky(gram_matrix)
    shape = snap_basis.shape[1:]

    def kapply(gap):
        product = jnp.dot(flat_basis, gap.reshape(-1), precision=lax.Precision.HIGHEST)
        coeffs = solve_small(factor, product)
        remainder = gap - jnp.dot(coeffs, flat_basis, precision=lax.Precision.HIGHEST).reshape(shape)
        padded = jnp.pad(remainder, ((0, 0), (1, 1), (0, 0), (0, 0)))
        return jnp.dot(coeffs, flat_images, precision=lax.Precision.HIGHEST).reshape(shape) + coarse_step(remainder, padded)
    gap = jnp.zeros(shape, jnp.float32)
    outputs = []
    for index in range(count):
        carried = kapply(gap)
        outputs.append(fine_ends[index] + prolong_field(carried))
        if index + 1 < count:
            gap = images[index] + carried - snap_basis[index + 1]
    return jnp.stack(outputs, axis=0)
```

```python
import functools

import jax
import jax.numpy as jnp
import numpy as np
from jax import lax
from jax.experimental import pallas as pl
from jax.experimental.pallas import tpu as pltpu
from jax.sharding import PartitionSpec as P

COARSEN = 4
SLICES = 16
DEVICES_Z = 16
NX, NY, NZ = 16, 32, 32
CX, CY = 64, 128
DEPTH = 8

kernel_near = 0.8
kernel_far = 0.2
diffusion = 0.08
coarse_rate = 0.1

ROWS = 24
HIGH = lax.Precision.HIGHEST


def real_fourier(n):
    x = np.arange(n)
    rows, freq = [np.full(n, 1.0 / np.sqrt(n))], [0]
    for k in range(1, n // 2):
        rows.append(np.sqrt(2.0 / n) * np.cos(2 * np.pi * k * x / n))
        rows.append(np.sqrt(2.0 / n) * np.sin(2 * np.pi * k * x / n))
        freq += [k, k]
    rows.append(((-1.0) ** x) / np.sqrt(n))
    freq.append(n // 2)
    return np.stack(rows), 2 * np.cos(2 * np.pi * np.array(freq) / n)


def constants():
    fx, ex = real_fourier(NX)
    fy, ey = real_fourier(NY)
    k = np.arange(1, NZ + 1)
    sz = np.sqrt(2.0 / (NZ + 1)) * np.sin(np.pi * np.outer(k, k) / (NZ + 1))
    ez = 2 * np.cos(np.pi * k / (NZ + 1))
    spread_x = np.repeat(np.eye(NX), COARSEN, axis=0)
    spread_y = np.repeat(np.eye(NY), COARSEN, axis=0)
    fwd_x = fx @ spread_x.T / 16.0
    fwd_y = spread_y @ fy.T / 4.0
    inv_x = spread_x @ fx.T
    inv_y = fy @ spread_y.T
    wide_fwd_y = np.zeros((3 * CY, 128))
    wide_inv_y = np.zeros((128, 3 * CY))
    for c in range(3):
        wide_fwd_y[c * CY : (c + 1) * CY, 32 * c : 32 * c + 32] = fwd_y
        wide_inv_y[32 * c : 32 * c + 32, c * CY : (c + 1) * CY] = inv_y
    fwd_z = np.zeros((2 * NZ, DEVICES_Z, 8))
    inv_z = np.zeros((DEVICES_Z, 8, NZ))
    for s in range(DEVICES_Z):
        for q in range(2):
            fwd_z[:NZ, s, q] = sz[:, 2 * s + q]
            fwd_z[NZ:, s, 2 + q] = sz[:, 2 * s + q]
            inv_z[s, q] = sz[2 * s + q]
        if s > 0:
            fwd_z[NZ:, s, 4] = sz[:, 2 * s - 1]
        if s < DEVICES_Z - 1:
            fwd_z[NZ:, s, 5] = sz[:, 2 * s + 2]
    full = 1.0 + coarse_rate * (ez[:, None] + ey[None, :] - 6.0)
    packed = np.zeros((ROWS, 128))
    for c in range(3):
        packed[:, 32 * c : 32 * c + 32] = full[:ROWS]
        packed[8 * c : 8 * c + 8, 96:] = full[ROWS:]
    f = lambda a: np.asarray(a, np.float32)
    return dict(
        fwd_x=f(fwd_x),
        wide_fwd_y=f(wide_fwd_y),
        inv_x=f(inv_x),
        wide_inv_y=f(wide_inv_y),
        fwd_z=f(fwd_z.reshape(2 * NZ, DEVICES_Z * 8)),
        inv_z=f(inv_z.reshape(DEVICES_Z * 8, NZ)),
        lam=f(packed),
        lam_full=f(np.tile(full, (1, 4))),
        lam_x=f(coarse_rate * ex),
    )


def dot(a, b, dims=((1,), (0,))):
    return lax.dot_general(
        a, b, (dims, ((), ())), precision=HIGH, preferred_element_type=jnp.float32
    )


def iota(shape, dim):
    return lax.broadcasted_iota(jnp.int32, shape, dim)


def fine_kernel(field_ref, strain_ref, fwd_x_ref, fwd_y_ref, fine_ref, coarse_ref, sums):
    sums[...] = jnp.zeros_like(sums)
    near = diffusion * kernel_near
    far = diffusion * kernel_far
    centre = 1.0 - 6.0 * (near + far)

    def plane(z, _):
        block = z // COARSEN
        up1, up2 = jnp.minimum(z + 1, DEPTH - 1), jnp.minimum(z + 2, DEPTH - 1)
        dn1, dn2 = jnp.maximum(z - 1, 0), jnp.maximum(z - 2, 0)
        w_up1 = jnp.where(z + 1 < DEPTH, near, 0.0).astype(jnp.float32)
        w_up2 = jnp.where(z + 2 < DEPTH, far, 0.0).astype(jnp.float32)
        w_dn1 = jnp.where(z >= 1, near, 0.0).astype(jnp.float32)
        w_dn2 = jnp.where(z >= 2, far, 0.0).astype(jnp.float32)
        comps = [field_ref[c, z] for c in range(3)]
        for c in range(3):
            f = comps[c]
            near_sum = pltpu.roll(f, 1, 0) + pltpu.roll(f, CX - 1, 0)
            near_sum = near_sum + pltpu.roll(f, 1, 1) + pltpu.roll(f, CY - 1, 1)
            far_sum = pltpu.roll(f, 2, 0) + pltpu.roll(f, CX - 2, 0)
            far_sum = far_sum + pltpu.roll(f, 2, 1) + pltpu.roll(f, CY - 2, 1)
            acc = centre * f + near * near_sum + far * far_sum
            acc = acc + w_up1 * field_ref[c, up1] + w_dn1 * field_ref[c, dn1]
            acc = acc + w_up2 * field_ref[c, up2] + w_dn2 * field_ref[c, dn2]
            for j in range(3):
                acc = acc + strain_ref[3 * c + j, z].astype(jnp.float32) * comps[j]
            fine_ref[c, z] = acc
            lanes = slice(c * CY, (c + 1) * CY)
            sums[block, :, lanes] += f
            sums[2 + block, :, lanes] += acc
        return 0

    lax.fori_loop(0, DEPTH, plane, 0)
    for c in range(3):
        lanes = slice(c * CY, (c + 1) * CY)
        sums[4, :, lanes] = diffusion * field_ref[c, 0] + far * field_ref[c, 1]
        sums[5, :, lanes] = diffusion * field_ref[c, DEPTH - 1] + far * field_ref[c, DEPTH - 2]
    along_x = [dot(fwd_x_ref[...], sums[q]) for q in range(6)]
    modes = dot(jnp.concatenate(along_x, axis=0), fwd_y_ref[...])
    for q in range(6):
        coarse_ref[:, q, :] = modes[NX * q : NX * (q + 1)]
    for q in range(6, 8):
        coarse_ref[:, q, :] = jnp.zeros((NX, 128), jnp.float32)


def depth_kernel(modes_ref, fwd_z_ref, lam_ref, lam_x_ref, out_ref):
    lam = lam_ref[...] + lam_x_ref[lax.axis_index("space")]
    both = dot(fwd_z_ref[...], modes_ref[...])
    basis = both[:NZ]
    defect = both[NZ:] - lam * basis
    group = iota((8, 128), 1) // 32
    tiles = []
    for v in (basis, defect):
        rest = v[ROWS:]
        for c in range(3):
            moved = pltpu.roll(rest, 96 - 32 * c, 1)
            tiles.append(jnp.where(group == 3, moved, v[8 * c : 8 * c + 8]))
    packed = jnp.concatenate(tiles, axis=0)
    for m in range(SLICES):
        out_ref[m] = packed


def gram_kernel(all_ref, lam_ref, lam_x_ref, out_ref):
    shift = lam_x_ref[lax.axis_index("space")]
    sub = iota((8, 128), 0)
    total = jnp.zeros((64, 88), jnp.float32)
    for r in range(0, ROWS, 2):
        left, right = [], []
        for row in (r, r + 1):
            b = all_ref[pl.ds(row, SLICES, stride=2 * ROWS), :]
            d = all_ref[pl.ds(ROWS + row, SLICES, stride=2 * ROWS), :]
            lam = lam_ref[row : row + 1, :] + shift
            lam2 = lam * lam
            lam4 = lam2 * lam2
            lam3 = lam2 * lam
            first = d[0:1] + lam * b[0:1]
            powers = jnp.where(sub == 0, 1.0, jnp.where(sub == 1, lam, jnp.where(sub == 2, lam2, lam3)))
            b4 = b * lam4
            b8 = b4 * lam4
            left.append(jnp.concatenate([b, b4, b8, b8 * lam4], axis=0))
            right.append(
                jnp.concatenate([d, d * lam, d * lam2, d * lam3, b, powers * first], axis=0)
            )
        total = total + dot(
            jnp.concatenate(left, axis=1), jnp.concatenate(right, axis=1), ((1,), (1,))
        )
    total = jnp.concatenate([total, jnp.zeros((64, 40), jnp.float32)], axis=1)
    a = [total[16 * i : 16 * i + 16] for i in range(4)]
    lane = iota((16, 128), 1)
    low = jnp.where(lane < 64, a[0], pltpu.roll(a[1], 64, 1))
    high = jnp.where(lane < 64, a[2], pltpu.roll(a[3], 64, 1))
    high = jnp.where((lane >= 96) & (lane < 112), pltpu.roll(a[0], 32, 1), high)
    for i in range(4):
        at = 112 + 4 * i
        high = jnp.where((lane >= at) & (lane < at + 4), pltpu.roll(a[i], (at - 80) % 128, 1), high)
    out_ref[:, :128] = low
    out_ref[:, 128:] = high


def solve_kernel(sums_ref, all_ref, inv_z_ref, lam_ref, lam_x_ref, out_ref):
    shift = lam_x_ref[lax.axis_index("space")]
    slice_index = lax.axis_index("tm")
    parts = sums_ref.shape[0]
    total = sums_ref[0]
    for i in range(1, parts):
        total = total + sums_ref[i]
    low, high = total[:, :128], total[:, 128:]
    lane = iota((16, 128), 1)
    sub = iota((16, 128), 0)
    for i in range(SLICES):
        column = high[:, 96 + i : 97 + i]
        scale = 1.0 / column[i : i + 1]
        factor = jnp.where(sub[:, :1] == i, column - 1.0, column) * scale
        low, high = low - factor * low[i : i + 1], high - factor * high[i : i + 1]
    diag = (lane & 15) == sub
    spread = (lane >> 3) == sub
    block = (iota((8, 128), 1) & 7) == iota((8, 128), 0)
    h_high = jnp.where(lane < 96, high, 0.0)
    acc_low = jnp.zeros((16, 128), jnp.float32)
    acc_high = jnp.zeros((16, 128), jnp.float32)
    first = jnp.where(iota((1, 128), 1) < 8, 1.0, 0.0)
    weights = [jnp.where(block, first, 0.0)]
    for k in range(1, SLICES):
        at = jnp.where(lane < 16, acc_low, 0.0) + jnp.where(lane == 112 + k - 1, high, 0.0)
        c = jnp.sum(at, axis=1, keepdims=True)
        weights.append(
            jnp.where(block, jnp.sum(jnp.where(spread, c, 0.0), axis=0, keepdims=True), 0.0)
        )
        if k < SLICES - 1:
            row = jnp.sum(jnp.where(diag, c, 0.0), axis=0, keepdims=True)
            shifted_low, shifted_high = pltpu.roll(acc_low, 112, 1), pltpu.roll(acc_high, 112, 1)
            if k > 1:
                acc_low = jnp.where(lane < 112, shifted_low, shifted_high)
                acc_high = jnp.where(lane < 112, shifted_high, 0.0)
            acc_low = acc_low + low * row
            acc_high = acc_high + h_high * row
    weights = jnp.concatenate(weights, axis=0)
    tiles = []
    for g in range(3):
        rows = slice(8 * g, 8 * g + 8)
        lam = lam_ref[rows] + shift
        d = all_ref[:, ROWS + 8 * g : ROWS + 8 * g + 8, :].reshape(128, 128)
        terms = dot(weights, d)
        b0 = all_ref[0, rows, :]
        value = terms[0:8] + lam * b0
        for k in range(1, SLICES):
            value = jnp.where(k <= slice_index, lam * value + terms[8 * k : 8 * k + 8], value)
        b_n = all_ref[slice_index, rows, :]
        d_n = all_ref[slice_index, ROWS + 8 * g : ROWS + 8 * g + 8, :]
        tiles.append(value - d_n - lam * b_n)
    group = iota((8, 128), 1) // 32
    rest = jnp.zeros((8, 128), jnp.float32)
    for c in range(3):
        rest = jnp.where(group == c, pltpu.roll(tiles[c], (32 * c - 96) % 128, 1), rest)
    out_ref[...] = dot(inv_z_ref[...], jnp.concatenate(tiles + [rest], axis=0))


def finish_kernel(fine_ref, below_ref, above_ref, modes_ref, inv_x_ref, inv_y_ref, out_ref):
    near = diffusion * kernel_near
    far = diffusion * kernel_far
    for q in range(2):
        along_x = dot(inv_x_ref[...], modes_ref[:, q, :])
        both = dot(along_x, inv_y_ref[...])
        for c in range(3):
            carried = both[:, c * CY : (c + 1) * CY]
            for k in range(COARSEN):
                z = COARSEN * q + k
                value = fine_ref[c, z] + carried
                if z == 0:
                    value = value + near * below_ref[c, 1] + far * below_ref[c, 0]
                if z == 1:
                    value = value + far * below_ref[c, 1]
                if z == DEPTH - 1:
                    value = value + near * above_ref[c, 0] + far * above_ref[c, 1]
                if z == DEPTH - 2:
                    value = value + far * above_ref[c, 0]
                out_ref[c, z] = value


VMEM = pl.BlockSpec(memory_space=pltpu.VMEM)
SMEM = pl.BlockSpec(memory_space=pltpu.SMEM)


def call(kernel, shapes, specs, scratch=()):
    out = jax.tree.map(lambda s: jax.ShapeDtypeStruct(s, jnp.float32), shapes, is_leaf=lambda s: isinstance(s, tuple) and isinstance(s[0], int))
    return pl.pallas_call(
        kernel,
        out_shape=out,
        in_specs=specs,
        out_specs=jax.tree.map(lambda _: VMEM, out),
        scratch_shapes=list(scratch),
    )


def local(starts, strain):
    con = constants()
    field, rates = starts[0], strain[0]
    count = lax.axis_size("space")
    below = lax.ppermute(field[:, DEPTH - 2 :], "space", [(i, i + 1) for i in range(count - 1)])
    above = lax.ppermute(field[:, :2], "space", [(i + 1, i) for i in range(count - 1)])

    fine, coarse = call(
        fine_kernel,
        [(3, DEPTH, CX, CY), (NX, 8, 128)],
        [VMEM] * 4,
        [pltpu.VMEM((6, CX, 3 * CY), jnp.float32)],
    )(field, rates, con["fwd_x"], con["wide_fwd_y"])
    coarse = lax.all_to_all(coarse, "space", 0, 0, tiled=True)
    mine = call(depth_kernel, (SLICES, 2 * ROWS, 128), [VMEM] * 3 + [SMEM])(
        coarse.reshape(128, 128), con["fwd_z"], con["lam_full"], con["lam_x"]
    )
    every = lax.all_to_all(mine, "tm", 0, 0, tiled=True)
    share = call(gram_kernel, (SLICES, 256), [VMEM] * 2 + [SMEM])(
        every.reshape(SLICES * 2 * ROWS, 128), con["lam"], con["lam_x"]
    )
    share = share + lax.ppermute(share, "space", [(i, i ^ 1) for i in range(count)])
    groups = [list(range(0, count, 2)), list(range(1, count, 2))]
    shares = lax.all_to_all(
        jnp.broadcast_to(share[None], (count // 2,) + share.shape),
        "space",
        0,
        0,
        axis_index_groups=groups,
        tiled=True,
    )
    carried = call(solve_kernel, (128, 128), [VMEM] * 4 + [SMEM])(
        shares, every, con["inv_z"], con["lam"], con["lam_x"]
    )
    carried = lax.all_to_all(carried.reshape(DEVICES_Z, 8, 128), "space", 0, 0, tiled=True)
    corrected = call(finish_kernel, (3, DEPTH, CX, CY), [VMEM] * 6)(
        fine, below, above, carried, con["inv_x"], con["wide_inv_y"]
    )
    return corrected[None]


def solution(mesh):
    return jax.shard_map(
        local,
        mesh=mesh,
        in_specs=(P("tm", None, "space", None, None), P("tm", None, "space", None, None)),
        out_specs=P("tm", None, "space", None, None),
        check_vma=False,
    )
```

```python
import functools

import jax
import jax.numpy as jnp
import numpy as np
from jax import lax
from jax.experimental import pallas as pl
from jax.experimental.pallas import tpu as pltpu
from jax.sharding import PartitionSpec as P

COARSEN = 4
SLICES = 16
DEVICES_Z = 16
NX, NY, NZ = 16, 32, 32
CX, CY = 64, 128
DEPTH = 8

kernel_near = 0.8
kernel_far = 0.2
diffusion = 0.08
coarse_rate = 0.1

ROWS = 24
HIGH = lax.Precision.HIGHEST


def real_fourier(n):
    x = np.arange(n)
    rows, freq = [np.full(n, 1.0 / np.sqrt(n))], [0]
    for k in range(1, n // 2):
        rows.append(np.sqrt(2.0 / n) * np.cos(2 * np.pi * k * x / n))
        rows.append(np.sqrt(2.0 / n) * np.sin(2 * np.pi * k * x / n))
        freq += [k, k]
    rows.append(((-1.0) ** x) / np.sqrt(n))
    freq.append(n // 2)
    return np.stack(rows), 2 * np.cos(2 * np.pi * np.array(freq) / n)


def constants():
    fx, ex = real_fourier(NX)
    fy, ey = real_fourier(NY)
    k = np.arange(1, NZ + 1)
    sz = np.sqrt(2.0 / (NZ + 1)) * np.sin(np.pi * np.outer(k, k) / (NZ + 1))
    ez = 2 * np.cos(np.pi * k / (NZ + 1))
    spread_x = np.repeat(np.eye(NX), COARSEN, axis=0)
    spread_y = np.repeat(np.eye(NY), COARSEN, axis=0)
    fwd_x = fx @ spread_x.T / 16.0
    fwd_y = spread_y @ fy.T / 4.0
    inv_x = spread_x @ fx.T
    inv_y = fy @ spread_y.T
    wide_fwd_y = np.zeros((3 * CY, 128))
    wide_inv_y = np.zeros((128, 3 * CY))
    for c in range(3):
        wide_fwd_y[c * CY : (c + 1) * CY, 32 * c : 32 * c + 32] = fwd_y
        wide_inv_y[32 * c : 32 * c + 32, c * CY : (c + 1) * CY] = inv_y
    fwd_z = np.zeros((2 * NZ, DEVICES_Z, 8))
    inv_z = np.zeros((DEVICES_Z, 8, NZ))
    for s in range(DEVICES_Z):
        for q in range(2):
            fwd_z[:NZ, s, q] = sz[:, 2 * s + q]
            fwd_z[NZ:, s, 2 + q] = sz[:, 2 * s + q]
            inv_z[s, q] = sz[2 * s + q]
        if s > 0:
            fwd_z[NZ:, s, 4] = sz[:, 2 * s - 1]
        if s < DEVICES_Z - 1:
            fwd_z[NZ:, s, 5] = sz[:, 2 * s + 2]
    full = 1.0 + coarse_rate * (ez[:, None] + ey[None, :] - 6.0)
    packed = np.zeros((ROWS, 128))
    for c in range(3):
        packed[:, 32 * c : 32 * c + 32] = full[:ROWS]
        packed[8 * c : 8 * c + 8, 96:] = full[ROWS:]
    f = lambda a: np.asarray(a, np.float32)
    return dict(
        fwd_x=f(fwd_x),
        wide_fwd_y=f(wide_fwd_y),
        inv_x=f(inv_x),
        wide_inv_y=f(wide_inv_y),
        fwd_z=f(fwd_z.reshape(2 * NZ, DEVICES_Z * 8)),
        inv_z=f(inv_z.reshape(DEVICES_Z * 8, NZ)),
        lam=f(packed),
        lam_full=f(np.tile(full, (1, 4))),
        lam_x=f(np.tile(coarse_rate * ex[:, None], (1, 128))),
    )


def dot(a, b, dims=((1,), (0,))):
    return lax.dot_general(
        a, b, (dims, ((), ())), precision=HIGH, preferred_element_type=jnp.float32
    )


def iota(shape, dim):
    return lax.broadcasted_iota(jnp.int32, shape, dim)


def around(f, width):
    total = pltpu.roll(f, width, 0) + pltpu.roll(f, CX - width, 0)
    return total + pltpu.roll(f, width, 1) + pltpu.roll(f, CY - width, 1)


def coarse_kernel(field_ref, strain_ref, fwd_x_ref, fwd_y_ref, coarse_ref, sums):
    near = diffusion * kernel_near
    far = diffusion * kernel_far

    def block(q, _):
        basis = [None] * 3
        stretch = [None] * 3
        for k in range(COARSEN):
            z = COARSEN * q + k
            comps = [field_ref[c, z] for c in range(3)]
            for c in range(3):
                acc = strain_ref[3 * c, z].astype(jnp.float32) * comps[0]
                for j in range(1, 3):
                    acc = acc + strain_ref[3 * c + j, z].astype(jnp.float32) * comps[j]
                stretch[c] = acc if k == 0 else stretch[c] + acc
                basis[c] = comps[c] if k == 0 else basis[c] + comps[c]
        for c in range(3):
            lanes = slice(c * CY, (c + 1) * CY)
            total = basis[c]
            sums[q, :, lanes] = total
            sums[2 + q, :, lanes] = (
                (1.0 - 4.0 * (near + far)) * total
                + stretch[c]
                + near * around(total, 1)
                + far * around(total, 2)
            )
        return 0

    lax.fori_loop(0, 2, block, 0)
    for c in range(3):
        lanes = slice(c * CY, (c + 1) * CY)
        low = [diffusion * field_ref[c, 4 * q] + far * field_ref[c, 4 * q + 1] for q in range(2)]
        high = [diffusion * field_ref[c, 4 * q + 3] + far * field_ref[c, 4 * q + 2] for q in range(2)]
        middle = low[1] - high[0]
        sums[2, :, lanes] += middle - low[0]
        sums[3, :, lanes] -= middle + high[1]
        sums[4, :, lanes] = low[0]
        sums[5, :, lanes] = high[1]
    along_x = [dot(fwd_x_ref[...], sums[q]) for q in range(6)]
    modes = dot(jnp.concatenate(along_x, axis=0), fwd_y_ref[...])
    for q in range(6):
        coarse_ref[:, q, :] = modes[NX * q : NX * (q + 1)]
    for q in range(6, 8):
        coarse_ref[:, q, :] = jnp.zeros((NX, 128), jnp.float32)


def fine_kernel(field_ref, strain_ref, below_ref, above_ref, fine_ref):
    near = diffusion * kernel_near
    far = diffusion * kernel_far
    centre = 1.0 - 6.0 * (near + far)

    def plane(z, _):
        up1, up2 = jnp.minimum(z + 1, DEPTH - 1), jnp.minimum(z + 2, DEPTH - 1)
        dn1, dn2 = jnp.maximum(z - 1, 0), jnp.maximum(z - 2, 0)
        w_up1 = jnp.where(z + 1 < DEPTH, near, 0.0).astype(jnp.float32)
        w_up2 = jnp.where(z + 2 < DEPTH, far, 0.0).astype(jnp.float32)
        w_dn1 = jnp.where(z >= 1, near, 0.0).astype(jnp.float32)
        w_dn2 = jnp.where(z >= 2, far, 0.0).astype(jnp.float32)
        comps = [field_ref[c, z] for c in range(3)]
        for c in range(3):
            f = comps[c]
            acc = centre * f + near * around(f, 1) + far * around(f, 2)
            acc = acc + w_up1 * field_ref[c, up1] + w_dn1 * field_ref[c, dn1]
            acc = acc + w_up2 * field_ref[c, up2] + w_dn2 * field_ref[c, dn2]
            for j in range(3):
                acc = acc + strain_ref[3 * c + j, z].astype(jnp.float32) * comps[j]
            fine_ref[c, z] = acc
        return 0

    lax.fori_loop(0, DEPTH, plane, 0)
    for c in range(3):
        fine_ref[c, 0] += near * below_ref[c, 1] + far * below_ref[c, 0]
        fine_ref[c, 1] += far * below_ref[c, 1]
        fine_ref[c, DEPTH - 2] += far * above_ref[c, 0]
        fine_ref[c, DEPTH - 1] += near * above_ref[c, 0] + far * above_ref[c, 1]


def depth_kernel(modes_ref, fwd_z_ref, lam_ref, lam_x_ref, out_ref):
    lam = lam_ref[...] + lam_x_ref[pl.ds(lax.axis_index("space"), 1), :]
    both = dot(fwd_z_ref[...], modes_ref[...])
    basis = both[:NZ]
    defect = both[NZ:] - lam * basis
    group = iota((8, 128), 1) // 32
    tiles = []
    for v in (basis, defect):
        rest = v[ROWS:]
        for c in range(3):
            moved = pltpu.roll(rest, 96 - 32 * c, 1)
            tiles.append(jnp.where(group == 3, moved, v[8 * c : 8 * c + 8]))
    packed = jnp.concatenate(tiles, axis=0)
    for m in range(SLICES):
        out_ref[m] = packed


def gram_kernel(all_ref, lam_ref, lam_x_ref, out_ref):
    shift = lam_x_ref[pl.ds(lax.axis_index("space"), 1), :]
    sub = iota((8, 128), 0)
    total = jnp.zeros((64, 88), jnp.float32)
    for r in range(0, ROWS, 2):
        left, right = [], []
        for row in (r, r + 1):
            b = all_ref[pl.ds(row, SLICES, stride=2 * ROWS), :]
            d = all_ref[pl.ds(ROWS + row, SLICES, stride=2 * ROWS), :]
            lam = lam_ref[row : row + 1, :] + shift
            lam2 = lam * lam
            lam4 = lam2 * lam2
            lam3 = lam2 * lam
            first = d[0:1] + lam * b[0:1]
            powers = jnp.where(sub == 0, 1.0, jnp.where(sub == 1, lam, jnp.where(sub == 2, lam2, lam3)))
            b4 = b * lam4
            b8 = b4 * lam4
            left.append(jnp.concatenate([b, b4, b8, b8 * lam4], axis=0))
            right.append(
                jnp.concatenate([d, d * lam, d * lam2, d * lam3, b, powers * first], axis=0)
            )
        total = total + dot(
            jnp.concatenate(left, axis=1), jnp.concatenate(right, axis=1), ((1,), (1,))
        )
    total = jnp.concatenate([total, jnp.zeros((64, 40), jnp.float32)], axis=1)
    a = [total[16 * i : 16 * i + 16] for i in range(4)]
    lane = iota((16, 128), 1)
    low = jnp.where(lane < 64, a[0], pltpu.roll(a[1], 64, 1))
    high = jnp.where(lane < 64, a[2], pltpu.roll(a[3], 64, 1))
    high = jnp.where((lane >= 96) & (lane < 112), pltpu.roll(a[0], 32, 1), high)
    for i in range(4):
        at = 112 + 4 * i
        high = jnp.where((lane >= at) & (lane < at + 4), pltpu.roll(a[i], (at - 80) % 128, 1), high)
    out_ref[:, :128] = low
    out_ref[:, 128:] = high


def solve_kernel(sums_ref, all_ref, inv_z_ref, lam_ref, lam_x_ref, out_ref):
    shift = lam_x_ref[pl.ds(lax.axis_index("space"), 1), :]
    slice_index = lax.axis_index("tm")
    parts = sums_ref.shape[0]
    total = sums_ref[0]
    for i in range(1, parts):
        total = total + sums_ref[i]
    low, high = total[:, :128], total[:, 128:]
    lane = iota((16, 128), 1)
    sub = iota((16, 128), 0)
    columns = [jnp.broadcast_to(high[:, 96 + i : 97 + i], (16, 128)) for i in range(SLICES)]
    for i in range(SLICES):
        column = columns[i]
        factor = jnp.where(sub == i, column - 1.0, column) * (1.0 / column[i : i + 1])
        for j in range(i + 1, SLICES):
            columns[j] = columns[j] - factor * columns[j][i : i + 1]
        low, high = low - factor * low[i : i + 1], high - factor * high[i : i + 1]

    def shifted(pair, by):
        rolled = [pltpu.roll(v, 128 - by, 1) for v in pair]
        inside = lane < 128 - by
        return jnp.where(inside, rolled[0], rolled[1]), jnp.where(inside, rolled[1], 0.0)

    diag = (lane & 15) == sub
    spread = (lane >> 3) == sub
    block = (iota((8, 128), 1) & 7) == iota((8, 128), 0)
    starts = [high, None]
    one = (low, jnp.where(lane < 96, high, 0.0))
    one_next = shifted(one, 16)
    twice = dot(low[:, :16], jnp.concatenate([low, high], axis=1))
    starts[1] = twice[:, 128:] + pltpu.roll(high, 127, 1)
    two = (twice[:, :128] + one_next[0], jnp.where(lane < 80, twice[:, 128:] + one_next[1], 0.0))
    two_next = shifted(two, 16)
    acc_one = acc_two = None
    first = jnp.where(iota((1, 128), 1) < 8, 1.0, 0.0)
    weights = [jnp.where(block, first, 0.0)]
    for n in range(0, SLICES, 2):
        found = []
        for acc, start in ((acc_one, starts[0]), (acc_two, starts[1])):
            if n == SLICES - 2 and found:
                break
            at = jnp.where(lane == 112 + n, start, 0.0)
            if n > 0:
                at = at + jnp.where(lane < 16, acc[0], 0.0)
            c = jnp.sum(at, axis=1, keepdims=True)
            found.append(c)
            weights.append(
                jnp.where(block, jnp.sum(jnp.where(spread, c, 0.0), axis=0, keepdims=True), 0.0)
            )
        if n < SLICES - 2:
            older, newer = [
                jnp.sum(jnp.where(diag, c, 0.0), axis=0, keepdims=True) for c in found
            ]
            grown_one = [a * newer + b * older for a, b in zip(one, one_next)]
            grown_two = [a * newer + b * older for a, b in zip(two, two_next)]
            if n > 0:
                grown_one = [a + b for a, b in zip(grown_one, shifted(acc_one, 32))]
                grown_two = [a + b for a, b in zip(grown_two, shifted(acc_two, 32))]
            acc_one, acc_two = grown_one, grown_two
    weights = jnp.concatenate(weights, axis=0)
    tiles = []
    for g in range(3):
        rows = slice(8 * g, 8 * g + 8)
        lam = lam_ref[rows] + shift
        d = all_ref[:, ROWS + 8 * g : ROWS + 8 * g + 8, :].reshape(128, 128)
        terms = dot(weights, d)
        b0 = all_ref[0, rows, :]
        value = terms[0:8] + lam * b0
        for k in range(1, SLICES):
            value = jnp.where(k <= slice_index, lam * value + terms[8 * k : 8 * k + 8], value)
        b_n = all_ref[slice_index, rows, :]
        d_n = all_ref[slice_index, ROWS + 8 * g : ROWS + 8 * g + 8, :]
        tiles.append(value - d_n - lam * b_n)
    group = iota((8, 128), 1) // 32
    rest = jnp.zeros((8, 128), jnp.float32)
    for c in range(3):
        rest = jnp.where(group == c, pltpu.roll(tiles[c], (32 * c - 96) % 128, 1), rest)
    out_ref[...] = dot(inv_z_ref[...], jnp.concatenate(tiles + [rest], axis=0))


def pair_kernel(mine_ref, other_ref, out_ref):
    total = mine_ref[...] + other_ref[...]
    for i in range(out_ref.shape[0]):
        out_ref[i] = total


def finish_kernel(fine_ref, modes_ref, inv_x_ref, inv_y_ref, out_hbm, out_ref, sem):
    copies = []
    for q in range(2):
        both = dot(dot(inv_x_ref[...], modes_ref[:, q, :]), inv_y_ref[...])
        for c in range(3):
            carried = both[:, c * CY : (c + 1) * CY]
            for k in range(COARSEN):
                z = COARSEN * q + k
                out_ref[c, z] = fine_ref[c, z] + carried
            planes = pl.ds(COARSEN * q, COARSEN)
            copy = pltpu.make_async_copy(
                out_ref.at[c, planes], out_hbm.at[c, planes], sem.at[q, c]
            )
            copy.start()
            copies.append(copy)
    for copy in copies:
        copy.wait()


VMEM = pl.BlockSpec(memory_space=pltpu.VMEM)
SMEM = pl.BlockSpec(memory_space=pltpu.SMEM)
HBM = pl.BlockSpec(memory_space=pltpu.HBM)


def fast(x):
    return pltpu.with_memory_space_constraint(x, pltpu.VMEM)


def call(kernel, outs, specs, scratch=(), out_specs=None):
    return pl.pallas_call(
        kernel,
        out_shape=outs,
        in_specs=specs,
        out_specs=VMEM if out_specs is None else out_specs,
        scratch_shapes=list(scratch),
    )


def near_array(*shape):
    return pltpu.VMEM(shape, jnp.float32)


def far_array(*shape):
    return jax.ShapeDtypeStruct(shape, jnp.float32)


def local(starts, strain):
    first = ("fwd_x", "wide_fwd_y")
    con = {k: v if k in first else fast(jnp.asarray(v)) for k, v in constants().items()}
    field, rates = starts[0], strain[0]
    count = lax.axis_size("space")

    coarse = call(
        coarse_kernel,
        near_array(NX, 8, 128),
        [VMEM] * 4,
        [pltpu.VMEM((6, CX, 3 * CY), jnp.float32)],
    )(field, rates, con["fwd_x"], con["wide_fwd_y"])
    coarse = lax.all_to_all(coarse, "space", 0, 0, tiled=True)
    mine = call(depth_kernel, near_array(SLICES, 2 * ROWS, 128), [VMEM] * 4)(
        fast(coarse.reshape(128, 128)), con["fwd_z"], con["lam_full"], con["lam_x"]
    )
    later, mine = lax.optimization_barrier((field, mine))
    every = lax.all_to_all(mine, "tm", 0, 0, tiled=True)
    below = lax.ppermute(later[:, DEPTH - 2 :], "space", [(i, i + 1) for i in range(count - 1)])
    above = lax.ppermute(later[:, :2], "space", [(i + 1, i) for i in range(count - 1)])
    share = call(gram_kernel, near_array(SLICES, 256), [VMEM] * 3)(
        fast(every.reshape(SLICES * 2 * ROWS, 128)), con["lam"], con["lam_x"]
    )
    fine = call(fine_kernel, near_array(*field.shape), [VMEM] * 4)(
        later, rates, fast(below), fast(above)
    )
    other = lax.ppermute(share, "space", [(i, i ^ 1) for i in range(count)])
    pair = call(pair_kernel, near_array(count // 2, *share.shape), [VMEM] * 2)(
        fast(share), fast(other)
    )
    groups = [list(range(0, count, 2)), list(range(1, count, 2))]
    shares = lax.all_to_all(pair, "space", 0, 0, axis_index_groups=groups, tiled=True)
    carried = call(solve_kernel, near_array(128, 128), [VMEM] * 5)(
        fast(shares), fast(every), con["inv_z"], con["lam"], con["lam_x"]
    )
    carried = lax.all_to_all(carried.reshape(DEVICES_Z, 8, 128), "space", 0, 0, tiled=True)
    corrected = call(
        finish_kernel,
        far_array(*field.shape),
        [VMEM] * 4,
        [pltpu.VMEM(field.shape, jnp.float32), pltpu.SemaphoreType.DMA((2, 3))],
        HBM,
    )(fast(fine), fast(carried), con["inv_x"], con["wide_inv_y"])
    return corrected[None]


def solution(mesh):
    return jax.shard_map(
        local,
        mesh=mesh,
        in_specs=(P("tm", None, "space", None, None), P("tm", None, "space", None, None)),
        out_specs=P("tm", None, "space", None, None),
        check_vma=False,
    )
```

```python
import functools

import jax
import jax.numpy as jnp
import numpy as np
from jax import lax
from jax.experimental import pallas as pl
from jax.experimental.pallas import tpu as pltpu
from jax.sharding import PartitionSpec as P

COARSEN = 4
SLICES = 16
DEVICES_Z = 16
NX, NY, NZ = 16, 32, 32
CX, CY = 64, 128
DEPTH = 8

kernel_near = 0.8
kernel_far = 0.2
diffusion = 0.08
coarse_rate = 0.1

ROWS = 24
HIGH = lax.Precision.HIGHEST


def real_fourier(n):
    x = np.arange(n)
    rows, freq = [np.full(n, 1.0 / np.sqrt(n))], [0]
    for k in range(1, n // 2):
        rows.append(np.sqrt(2.0 / n) * np.cos(2 * np.pi * k * x / n))
        rows.append(np.sqrt(2.0 / n) * np.sin(2 * np.pi * k * x / n))
        freq += [k, k]
    rows.append(((-1.0) ** x) / np.sqrt(n))
    freq.append(n // 2)
    return np.stack(rows), 2 * np.cos(2 * np.pi * np.array(freq) / n)


def constants():
    fx, ex = real_fourier(NX)
    fy, ey = real_fourier(NY)
    k = np.arange(1, NZ + 1)
    sz = np.sqrt(2.0 / (NZ + 1)) * np.sin(np.pi * np.outer(k, k) / (NZ + 1))
    ez = 2 * np.cos(np.pi * k / (NZ + 1))
    spread_x = np.repeat(np.eye(NX), COARSEN, axis=0)
    spread_y = np.repeat(np.eye(NY), COARSEN, axis=0)
    fwd_x = fx / 16.0
    fwd_y = spread_y @ fy.T / 4.0
    inv_x = spread_x @ fx.T
    inv_y = fy @ spread_y.T
    wide_fwd_y = np.zeros((3 * CY, 128))
    wide_inv_y = np.zeros((128, 3 * CY))
    for c in range(3):
        wide_fwd_y[c * CY : (c + 1) * CY, 32 * c : 32 * c + 32] = fwd_y
        wide_inv_y[32 * c : 32 * c + 32, c * CY : (c + 1) * CY] = inv_y
    fwd_z = np.zeros((2 * NZ, DEVICES_Z, 8))
    for s in range(DEVICES_Z):
        for q in range(2):
            fwd_z[:NZ, s, q] = sz[:, 2 * s + q]
            fwd_z[NZ:, s, 2 + q] = sz[:, 2 * s + q]
        if s > 0:
            fwd_z[NZ:, s, 4] = sz[:, 2 * s - 1]
        if s < DEVICES_Z - 1:
            fwd_z[NZ:, s, 5] = sz[:, 2 * s + 2]
    full = 1.0 + coarse_rate * (ez[:, None] + ey[None, :] - 6.0)
    packed = np.zeros((ROWS, 128))
    for c in range(3):
        packed[:, 32 * c : 32 * c + 32] = full[:ROWS]
        packed[8 * c : 8 * c + 8, 96:] = full[ROWS:]
    f = lambda a: np.asarray(a, np.float32)
    return dict(
        fwd_x=f(fwd_x),
        wide_fwd_y=f(wide_fwd_y),
        inv_x=f(inv_x),
        wide_inv_y=f(wide_inv_y),
        fwd_z=f(fwd_z.reshape(2 * NZ, DEVICES_Z * 8)),
        inv_z=f(sz),
        lam=f(packed),
        lam_full=f(np.tile(full, (1, 4))),
        lam_x=f(np.tile(coarse_rate * ex[:, None], (1, 128))),
    )


def dot(a, b, dims=((1,), (0,))):
    return lax.dot_general(
        a, b, (dims, ((), ())), precision=HIGH, preferred_element_type=jnp.float32
    )


def iota(shape, dim):
    return lax.broadcasted_iota(jnp.int32, shape, dim)


def around(f, width):
    total = pltpu.roll(f, width, 0) + pltpu.roll(f, CX - width, 0)
    return total + pltpu.roll(f, width, 1) + pltpu.roll(f, CY - width, 1)


def coarse_kernel(
    field_hbm, strain_hbm, fwd_x_hbm, fwd_y_hbm, coarse_ref,
    field_ref, strain_ref, fwd_x_ref, fwd_y_ref, sums, sem,
):
    near = diffusion * kernel_near
    far = diffusion * kernel_far

    def arrays(q):
        planes = pl.ds(COARSEN * q, COARSEN)
        return [
            pltpu.make_async_copy(field_hbm.at[:, planes], field_ref.at[:, planes], sem.at[q, 0]),
            pltpu.make_async_copy(strain_hbm.at[:, planes], strain_ref.at[:, planes], sem.at[q, 1]),
        ]

    tables = [
        pltpu.make_async_copy(fwd_x_hbm, fwd_x_ref, sem.at[2, 0]),
        pltpu.make_async_copy(fwd_y_hbm, fwd_y_ref, sem.at[2, 1]),
    ]
    for copy in arrays(0) + arrays(1) + tables:
        copy.start()

    def block(q, _):
        for copy in arrays(q):
            copy.wait()
        basis = [None] * 3
        stretch = [None] * 3
        for k in range(COARSEN):
            z = COARSEN * q + k
            comps = [field_ref[c, z] for c in range(3)]
            for c in range(3):
                acc = strain_ref[3 * c, z].astype(jnp.float32) * comps[0]
                for j in range(1, 3):
                    acc = acc + strain_ref[3 * c + j, z].astype(jnp.float32) * comps[j]
                stretch[c] = acc if k == 0 else stretch[c] + acc
                basis[c] = comps[c] if k == 0 else basis[c] + comps[c]
        for c in range(3):
            total = basis[c]
            sums[q, c] = total
            sums[2 + q, c] = (
                (1.0 - 4.0 * (near + far)) * total
                + stretch[c]
                + near * around(total, 1)
                + far * around(total, 2)
            )
        return 0

    lax.fori_loop(0, 2, block, 0)
    for c in range(3):
        low = [diffusion * field_ref[c, 4 * q] + far * field_ref[c, 4 * q + 1] for q in range(2)]
        high = [diffusion * field_ref[c, 4 * q + 3] + far * field_ref[c, 4 * q + 2] for q in range(2)]
        middle = low[1] - high[0]
        sums[2, c] += middle - low[0]
        sums[3, c] -= middle + high[1]
        sums[4, c] = low[0]
        sums[5, c] = high[1]
    for copy in tables:
        copy.wait()
    along_x = []
    for q in range(6):
        wide = []
        for c in range(3):
            rows = [sums[q, c, pl.ds(k, NX, stride=COARSEN), :] for k in range(COARSEN)]
            wide.append((rows[0] + rows[1]) + (rows[2] + rows[3]))
        along_x.append(dot(fwd_x_ref[...], jnp.concatenate(wide, axis=1)))
    modes = dot(jnp.concatenate(along_x, axis=0), fwd_y_ref[...])
    for q in range(6):
        coarse_ref[:, q, :] = modes[NX * q : NX * (q + 1)]
    for q in range(6, 8):
        coarse_ref[:, q, :] = jnp.zeros((NX, 128), jnp.float32)


def fine_kernel(field_ref, strain_ref, below_ref, above_ref, fine_ref):
    near = diffusion * kernel_near
    far = diffusion * kernel_far
    centre = 1.0 - 6.0 * (near + far)

    def plane(z, _):
        up1, up2 = jnp.minimum(z + 1, DEPTH - 1), jnp.minimum(z + 2, DEPTH - 1)
        dn1, dn2 = jnp.maximum(z - 1, 0), jnp.maximum(z - 2, 0)
        w_up1 = jnp.where(z + 1 < DEPTH, near, 0.0).astype(jnp.float32)
        w_up2 = jnp.where(z + 2 < DEPTH, far, 0.0).astype(jnp.float32)
        w_dn1 = jnp.where(z >= 1, near, 0.0).astype(jnp.float32)
        w_dn2 = jnp.where(z >= 2, far, 0.0).astype(jnp.float32)
        comps = [field_ref[c, z] for c in range(3)]
        for c in range(3):
            f = comps[c]
            acc = centre * f + near * around(f, 1) + far * around(f, 2)
            acc = acc + w_up1 * field_ref[c, up1] + w_dn1 * field_ref[c, dn1]
            acc = acc + w_up2 * field_ref[c, up2] + w_dn2 * field_ref[c, dn2]
            for j in range(3):
                acc = acc + strain_ref[3 * c + j, z].astype(jnp.float32) * comps[j]
            fine_ref[c, z] = acc
        return 0

    lax.fori_loop(0, DEPTH, plane, 0)
    for c in range(3):
        fine_ref[c, 0] += near * below_ref[c, 1] + far * below_ref[c, 0]
        fine_ref[c, 1] += far * below_ref[c, 1]
        fine_ref[c, DEPTH - 2] += far * above_ref[c, 0]
        fine_ref[c, DEPTH - 1] += near * above_ref[c, 0] + far * above_ref[c, 1]


def depth_kernel(modes_ref, fwd_z_ref, lam_ref, lam_x_ref, out_ref):
    lam = lam_ref[...] + lam_x_ref[pl.ds(lax.axis_index("space"), 1), :]
    both = dot(fwd_z_ref[...], modes_ref[...])
    basis = both[:NZ]
    defect = both[NZ:] - lam * basis
    group = iota((8, 128), 1) // 32
    tiles = []
    for v in (basis, defect):
        rest = v[ROWS:]
        for c in range(3):
            moved = pltpu.roll(rest, 96 - 32 * c, 1)
            tiles.append(jnp.where(group == 3, moved, v[8 * c : 8 * c + 8]))
    packed = jnp.concatenate(tiles, axis=0)
    for m in range(SLICES):
        out_ref[m] = packed


def gram_kernel(all_ref, lam_ref, lam_x_ref, out_ref):
    shift = lam_x_ref[pl.ds(lax.axis_index("space"), 1), :]
    sub = iota((8, 128), 0)
    total = jnp.zeros((64, 88), jnp.float32)
    for r in range(0, ROWS, 2):
        left, right = [], []
        for row in (r, r + 1):
            b = all_ref[pl.ds(row, SLICES, stride=2 * ROWS), :]
            d = all_ref[pl.ds(ROWS + row, SLICES, stride=2 * ROWS), :]
            lam = lam_ref[row : row + 1, :] + shift
            lam2 = lam * lam
            lam4 = lam2 * lam2
            lam3 = lam2 * lam
            first = d[0:1] + lam * b[0:1]
            powers = jnp.where(sub == 0, 1.0, jnp.where(sub == 1, lam, jnp.where(sub == 2, lam2, lam3)))
            b4 = b * lam4
            b8 = b4 * lam4
            left.append(jnp.concatenate([b, b4, b8, b8 * lam4], axis=0))
            right.append(
                jnp.concatenate([d, d * lam, d * lam2, d * lam3, b, powers * first], axis=0)
            )
        total = total + dot(
            jnp.concatenate(left, axis=1), jnp.concatenate(right, axis=1), ((1,), (1,))
        )
    total = jnp.concatenate([total, jnp.zeros((64, 40), jnp.float32)], axis=1)
    a = [total[16 * i : 16 * i + 16] for i in range(4)]
    lane = iota((16, 128), 1)
    low = jnp.where(lane < 64, a[0], pltpu.roll(a[1], 64, 1))
    high = jnp.where(lane < 64, a[2], pltpu.roll(a[3], 64, 1))
    high = jnp.where((lane >= 96) & (lane < 112), pltpu.roll(a[0], 32, 1), high)
    for i in range(4):
        at = 112 + 4 * i
        high = jnp.where((lane >= at) & (lane < at + 4), pltpu.roll(a[i], (at - 80) % 128, 1), high)
    out_ref[:, :128] = low
    out_ref[:, 128:] = high


def solve_kernel(sums_ref, all_ref, inv_z_ref, lam_ref, lam_x_ref, out_ref):
    shift = lam_x_ref[pl.ds(lax.axis_index("space"), 1), :]
    slice_index = lax.axis_index("tm")
    parts = sums_ref.shape[0]
    total = sums_ref[0]
    for i in range(1, parts):
        total = total + sums_ref[i]
    low, high = total[:, :128], total[:, 128:]
    lane = iota((16, 128), 1)
    sub = iota((16, 128), 0)
    columns = [jnp.broadcast_to(high[:, 96 + i : 97 + i], (16, 128)) for i in range(SLICES)]
    for i in range(SLICES):
        column = columns[i]
        factor = jnp.where(sub == i, column - 1.0, column) * (1.0 / column[i : i + 1])
        for j in range(i + 1, SLICES):
            columns[j] = columns[j] - factor * columns[j][i : i + 1]
        low, high = low - factor * low[i : i + 1], high - factor * high[i : i + 1]

    def shifted(pair, by):
        rolled = [pltpu.roll(v, 128 - by, 1) for v in pair]
        inside = lane < 128 - by
        return jnp.where(inside, rolled[0], rolled[1]), jnp.where(inside, rolled[1], 0.0)

    diag = (lane & 15) == sub
    spread = (lane >> 3) == sub
    block = (iota((8, 128), 1) & 7) == iota((8, 128), 0)
    starts = [high, None]
    one = (low, jnp.where(lane < 96, high, 0.0))
    one_next = shifted(one, 16)
    twice = dot(low[:, :16], jnp.concatenate([low, high], axis=1))
    starts[1] = twice[:, 128:] + pltpu.roll(high, 127, 1)
    two = (twice[:, :128] + one_next[0], jnp.where(lane < 80, twice[:, 128:] + one_next[1], 0.0))
    two_next = shifted(two, 16)
    acc_one = acc_two = None
    first = jnp.where(iota((1, 128), 1) < 8, 1.0, 0.0)
    weights = [jnp.where(block, first, 0.0)]
    for n in range(0, SLICES, 2):
        found = []
        for acc, start in ((acc_one, starts[0]), (acc_two, starts[1])):
            if n == SLICES - 2 and found:
                break
            at = jnp.where(lane == 112 + n, start, 0.0)
            if n > 0:
                at = at + jnp.where(lane < 16, acc[0], 0.0)
            c = jnp.sum(at, axis=1, keepdims=True)
            found.append(c)
            weights.append(
                jnp.where(block, jnp.sum(jnp.where(spread, c, 0.0), axis=0, keepdims=True), 0.0)
            )
        if n < SLICES - 2:
            older, newer = [
                jnp.sum(jnp.where(diag, c, 0.0), axis=0, keepdims=True) for c in found
            ]
            grown_one = [a * newer + b * older for a, b in zip(one, one_next)]
            grown_two = [a * newer + b * older for a, b in zip(two, two_next)]
            if n > 0:
                grown_one = [a + b for a, b in zip(grown_one, shifted(acc_one, 32))]
                grown_two = [a + b for a, b in zip(grown_two, shifted(acc_two, 32))]
            acc_one, acc_two = grown_one, grown_two
    weights = jnp.concatenate(weights, axis=0)
    tiles = []
    for g in range(3):
        rows = slice(8 * g, 8 * g + 8)
        lam = lam_ref[rows] + shift
        d = all_ref[:, ROWS + 8 * g : ROWS + 8 * g + 8, :].reshape(128, 128)
        terms = dot(weights, d)
        b0 = all_ref[0, rows, :]
        value = terms[0:8] + lam * b0
        for k in range(1, SLICES):
            value = jnp.where(k <= slice_index, lam * value + terms[8 * k : 8 * k + 8], value)
        b_n = all_ref[slice_index, rows, :]
        d_n = all_ref[slice_index, ROWS + 8 * g : ROWS + 8 * g + 8, :]
        tiles.append(value - d_n - lam * b_n)
    group = iota((8, 128), 1) // 32
    rest = jnp.zeros((8, 128), jnp.float32)
    for c in range(3):
        rest = jnp.where(group == c, pltpu.roll(tiles[c], (32 * c - 96) % 128, 1), rest)
    planes = dot(inv_z_ref[...], jnp.concatenate(tiles + [rest], axis=0))
    for s in range(DEVICES_Z):
        out_ref[s] = planes[2 * s : 2 * s + 2]


def pair_kernel(mine_ref, other_ref, out_ref):
    total = mine_ref[...] + other_ref[...]
    for i in range(out_ref.shape[0]):
        out_ref[i] = total


def finish_kernel(fine_ref, modes_ref, inv_x_ref, inv_y_ref, out_hbm, out_ref, sem):
    copies = []
    for q in range(2):
        both = dot(dot(inv_x_ref[...], modes_ref[:, q, :]), inv_y_ref[...])
        for c in range(3):
            carried = both[:, c * CY : (c + 1) * CY]
            for k in range(COARSEN):
                z = COARSEN * q + k
                out_ref[c, z] = fine_ref[c, z] + carried
            planes = pl.ds(COARSEN * q, COARSEN)
            copy = pltpu.make_async_copy(
                out_ref.at[c, planes], out_hbm.at[c, planes], sem.at[q, c]
            )
            copy.start()
            copies.append(copy)
    for copy in copies:
        copy.wait()


VMEM = pl.BlockSpec(memory_space=pltpu.VMEM)
SMEM = pl.BlockSpec(memory_space=pltpu.SMEM)
HBM = pl.BlockSpec(memory_space=pltpu.HBM)


def fast(x):
    return pltpu.with_memory_space_constraint(x, pltpu.VMEM)


def call(kernel, outs, specs, scratch=(), out_specs=None):
    return pl.pallas_call(
        kernel,
        out_shape=outs,
        in_specs=specs,
        out_specs=VMEM if out_specs is None else out_specs,
        scratch_shapes=list(scratch),
    )


def near_array(*shape):
    return pltpu.VMEM(shape, jnp.float32)


def far_array(*shape):
    return jax.ShapeDtypeStruct(shape, jnp.float32)


def local(starts, strain):
    first = ("fwd_x", "wide_fwd_y")
    con = {k: v if k in first else fast(jnp.asarray(v)) for k, v in constants().items()}
    field, rates = starts[0], strain[0]
    count = lax.axis_size("space")

    coarse = call(
        coarse_kernel,
        near_array(NX, 8, 128),
        [HBM] * 4,
        [
            pltpu.VMEM(field.shape, jnp.float32),
            pltpu.VMEM(rates.shape, jnp.bfloat16),
            pltpu.VMEM((NX, NX), jnp.float32),
            pltpu.VMEM((3 * CY, 128), jnp.float32),
            pltpu.VMEM((6, 3, CX, CY), jnp.float32),
            pltpu.SemaphoreType.DMA((3, 2)),
        ],
    )(field, rates, con["fwd_x"], con["wide_fwd_y"])
    coarse = lax.all_to_all(coarse, "space", 0, 0, tiled=True)
    mine = call(depth_kernel, near_array(SLICES, 2 * ROWS, 128), [VMEM] * 4)(
        fast(coarse.reshape(128, 128)), con["fwd_z"], con["lam_full"], con["lam_x"]
    )
    later, mine = lax.optimization_barrier((field, mine))
    every = lax.all_to_all(mine, "tm", 0, 0, tiled=True)
    below = lax.ppermute(later[:, DEPTH - 2 :], "space", [(i, i + 1) for i in range(count - 1)])
    above = lax.ppermute(later[:, :2], "space", [(i + 1, i) for i in range(count - 1)])
    share = call(gram_kernel, near_array(SLICES, 256), [VMEM] * 3)(
        fast(every.reshape(SLICES * 2 * ROWS, 128)), con["lam"], con["lam_x"]
    )
    fine = call(fine_kernel, near_array(*field.shape), [VMEM] * 4)(
        later, rates, fast(below), fast(above)
    )
    other = lax.ppermute(share, "space", [(i, i ^ 1) for i in range(count)])
    pair = call(pair_kernel, near_array(count // 2, *share.shape), [VMEM] * 2)(
        fast(share), fast(other)
    )
    groups = [list(range(0, count, 2)), list(range(1, count, 2))]
    shares = lax.all_to_all(pair, "space", 0, 0, axis_index_groups=groups, tiled=True)
    carried = call(solve_kernel, near_array(DEVICES_Z, 2, 128), [VMEM] * 5)(
        fast(shares), fast(every), con["inv_z"], con["lam"], con["lam_x"]
    )
    carried = lax.all_to_all(carried, "space", 0, 0, tiled=True)
    corrected = call(
        finish_kernel,
        far_array(*field.shape),
        [VMEM] * 4,
        [pltpu.VMEM(field.shape, jnp.float32), pltpu.SemaphoreType.DMA((2, 3))],
        HBM,
    )(fast(fine), fast(carried), con["inv_x"], con["wide_inv_y"])
    return corrected[None]


def solution(mesh):
    return jax.shard_map(
        local,
        mesh=mesh,
        in_specs=(P("tm", None, "space", None, None), P("tm", None, "space", None, None)),
        out_specs=P("tm", None, "space", None, None),
        check_vma=False,
    )
```

```python
import functools

import jax
import jax.numpy as jnp
import numpy as np
from jax import lax
from jax.experimental import pallas as pl
from jax.experimental.pallas import tpu as pltpu
from jax.sharding import PartitionSpec as P

COARSEN = 4
SLICES = 16
DEVICES_Z = 16
NX, NY, NZ = 16, 32, 32
CX, CY = 64, 128
DEPTH = 8

kernel_near = 0.8
kernel_far = 0.2
diffusion = 0.08
coarse_rate = 0.1

ROWS = 24
HIGH = lax.Precision.HIGHEST


def real_fourier(n):
    x = np.arange(n)
    rows, freq = [np.full(n, 1.0 / np.sqrt(n))], [0]
    for k in range(1, n // 2):
        rows.append(np.sqrt(2.0 / n) * np.cos(2 * np.pi * k * x / n))
        rows.append(np.sqrt(2.0 / n) * np.sin(2 * np.pi * k * x / n))
        freq += [k, k]
    rows.append(((-1.0) ** x) / np.sqrt(n))
    freq.append(n // 2)
    return np.stack(rows), 2 * np.cos(2 * np.pi * np.array(freq) / n)


def constants():
    fx, ex = real_fourier(NX)
    fy, ey = real_fourier(NY)
    k = np.arange(1, NZ + 1)
    sz = np.sqrt(2.0 / (NZ + 1)) * np.sin(np.pi * np.outer(k, k) / (NZ + 1))
    ez = 2 * np.cos(np.pi * k / (NZ + 1))
    spread_x = np.repeat(np.eye(NX), COARSEN, axis=0)
    spread_y = np.repeat(np.eye(NY), COARSEN, axis=0)
    fwd_x = fx / 16.0
    fwd_y = spread_y @ fy.T / 4.0
    inv_x = spread_x @ fx.T
    inv_y = fy @ spread_y.T
    wide_fwd_y = np.zeros((3 * CY, 128))
    wide_inv_y = np.zeros((128, 3 * CY))
    for c in range(3):
        wide_fwd_y[c * CY : (c + 1) * CY, 32 * c : 32 * c + 32] = fwd_y
        wide_inv_y[32 * c : 32 * c + 32, c * CY : (c + 1) * CY] = inv_y
    fwd_z = np.zeros((2 * NZ, DEVICES_Z, 8))
    for s in range(DEVICES_Z):
        for q in range(2):
            fwd_z[:NZ, s, q] = sz[:, 2 * s + q]
            fwd_z[NZ:, s, 2 + q] = sz[:, 2 * s + q]
        if s > 0:
            fwd_z[NZ:, s, 4] = sz[:, 2 * s - 1]
        if s < DEVICES_Z - 1:
            fwd_z[NZ:, s, 5] = sz[:, 2 * s + 2]
    full = 1.0 + coarse_rate * (ez[:, None] + ey[None, :] - 6.0)
    packed = np.zeros((ROWS, 128))
    for c in range(3):
        packed[:, 32 * c : 32 * c + 32] = full[:ROWS]
        packed[8 * c : 8 * c + 8, 96:] = full[ROWS:]
    f = lambda a: np.asarray(a, np.float32)
    return dict(
        fwd_x=f(fwd_x),
        wide_fwd_y=f(wide_fwd_y),
        inv_x=f(inv_x),
        wide_inv_y=f(wide_inv_y),
        fwd_z=f(fwd_z.reshape(2 * NZ, DEVICES_Z * 8)),
        inv_z=f(sz),
        lam=f(packed),
        lam_full=f(np.tile(full, (1, 4))),
        lam_x=f(np.tile(coarse_rate * ex[:, None], (1, 128))),
    )


def dot(a, b, dims=((1,), (0,))):
    return lax.dot_general(
        a, b, (dims, ((), ())), precision=HIGH, preferred_element_type=jnp.float32
    )


def halves(x):
    high = x.astype(jnp.bfloat16)
    return high, (x - high.astype(jnp.float32)).astype(jnp.bfloat16)


def dot_halves(a, b, dims=((1,), (0,))):
    def part(x, y):
        return lax.dot_general(x, y, (dims, ((), ())), preferred_element_type=jnp.float32)

    (a_high, a_low), (b_high, b_low) = halves(a), halves(b)
    return part(a_high, b_high) + (part(a_high, b_low) + part(a_low, b_high))


def iota(shape, dim):
    return lax.broadcasted_iota(jnp.int32, shape, dim)


def around(f, width):
    total = pltpu.roll(f, width, 0) + pltpu.roll(f, CX - width, 0)
    return total + pltpu.roll(f, width, 1) + pltpu.roll(f, CY - width, 1)


def coarse_kernel(
    field_hbm, strain_hbm, fwd_x_hbm, fwd_y_hbm, coarse_ref,
    field_ref, strain_ref, fwd_x_ref, fwd_y_ref, sums, sem,
):
    near = diffusion * kernel_near
    far = diffusion * kernel_far

    def arrays(q):
        planes = pl.ds(COARSEN * q, COARSEN)
        return [
            pltpu.make_async_copy(field_hbm.at[:, planes], field_ref.at[:, planes], sem.at[q, 0]),
            pltpu.make_async_copy(strain_hbm.at[:, planes], strain_ref.at[:, planes], sem.at[q, 1]),
        ]

    tables = [
        pltpu.make_async_copy(fwd_x_hbm, fwd_x_ref, sem.at[2, 0]),
        pltpu.make_async_copy(fwd_y_hbm, fwd_y_ref, sem.at[2, 1]),
    ]
    for copy in arrays(0) + arrays(1) + tables:
        copy.start()

    def block(q, _):
        for copy in arrays(q):
            copy.wait()
        basis = [None] * 3
        stretch = [None] * 3
        for k in range(COARSEN):
            z = COARSEN * q + k
            comps = [field_ref[c, z] for c in range(3)]
            for c in range(3):
                acc = strain_ref[3 * c, z].astype(jnp.float32) * comps[0]
                for j in range(1, 3):
                    acc = acc + strain_ref[3 * c + j, z].astype(jnp.float32) * comps[j]
                stretch[c] = acc if k == 0 else stretch[c] + acc
                basis[c] = comps[c] if k == 0 else basis[c] + comps[c]
        for c in range(3):
            total = basis[c]
            sums[q, c] = total
            sums[2 + q, c] = (
                (1.0 - 4.0 * (near + far)) * total
                + stretch[c]
                + near * around(total, 1)
                + far * around(total, 2)
            )
        return 0

    lax.fori_loop(0, 2, block, 0)
    for c in range(3):
        low = [diffusion * field_ref[c, 4 * q] + far * field_ref[c, 4 * q + 1] for q in range(2)]
        high = [diffusion * field_ref[c, 4 * q + 3] + far * field_ref[c, 4 * q + 2] for q in range(2)]
        middle = low[1] - high[0]
        sums[2, c] += middle - low[0]
        sums[3, c] -= middle + high[1]
        sums[4, c] = low[0]
        sums[5, c] = high[1]
    for copy in tables:
        copy.wait()
    along_x = []
    for q in range(6):
        wide = []
        for c in range(3):
            rows = [sums[q, c, pl.ds(k, NX, stride=COARSEN), :] for k in range(COARSEN)]
            wide.append((rows[0] + rows[1]) + (rows[2] + rows[3]))
        along_x.append(dot(fwd_x_ref[...], jnp.concatenate(wide, axis=1)))
    modes = dot(jnp.concatenate(along_x, axis=0), fwd_y_ref[...])
    for q in range(6):
        coarse_ref[:, q, :] = modes[NX * q : NX * (q + 1)]
    for q in range(6, 8):
        coarse_ref[:, q, :] = jnp.zeros((NX, 128), jnp.float32)


def fine_kernel(field_ref, strain_ref, below_ref, above_ref, fine_ref):
    near = diffusion * kernel_near
    far = diffusion * kernel_far
    centre = 1.0 - 6.0 * (near + far)

    def plane(z, _):
        up1, up2 = jnp.minimum(z + 1, DEPTH - 1), jnp.minimum(z + 2, DEPTH - 1)
        dn1, dn2 = jnp.maximum(z - 1, 0), jnp.maximum(z - 2, 0)
        w_up1 = jnp.where(z + 1 < DEPTH, near, 0.0).astype(jnp.float32)
        w_up2 = jnp.where(z + 2 < DEPTH, far, 0.0).astype(jnp.float32)
        w_dn1 = jnp.where(z >= 1, near, 0.0).astype(jnp.float32)
        w_dn2 = jnp.where(z >= 2, far, 0.0).astype(jnp.float32)
        comps = [field_ref[c, z] for c in range(3)]
        for c in range(3):
            f = comps[c]
            acc = centre * f + near * around(f, 1) + far * around(f, 2)
            acc = acc + w_up1 * field_ref[c, up1] + w_dn1 * field_ref[c, dn1]
            acc = acc + w_up2 * field_ref[c, up2] + w_dn2 * field_ref[c, dn2]
            for j in range(3):
                acc = acc + strain_ref[3 * c + j, z].astype(jnp.float32) * comps[j]
            fine_ref[c, z] = acc
        return 0

    lax.fori_loop(0, DEPTH, plane, 0)
    for c in range(3):
        fine_ref[c, 0] += near * below_ref[c, 1] + far * below_ref[c, 0]
        fine_ref[c, 1] += far * below_ref[c, 1]
        fine_ref[c, DEPTH - 2] += far * above_ref[c, 0]
        fine_ref[c, DEPTH - 1] += near * above_ref[c, 0] + far * above_ref[c, 1]


def depth_kernel(modes_ref, fwd_z_ref, lam_ref, lam_x_ref, out_ref):
    lam = lam_ref[...] + lam_x_ref[pl.ds(lax.axis_index("space"), 1), :]
    both = dot(fwd_z_ref[...], modes_ref[...])
    basis = both[:NZ]
    defect = both[NZ:] - lam * basis
    group = iota((8, 128), 1) // 32
    tiles = []
    for v in (basis, defect):
        rest = v[ROWS:]
        for c in range(3):
            moved = pltpu.roll(rest, 96 - 32 * c, 1)
            tiles.append(jnp.where(group == 3, moved, v[8 * c : 8 * c + 8]))
    packed = jnp.concatenate(tiles, axis=0)
    for m in range(SLICES):
        out_ref[m] = packed


def gram_kernel(all_ref, lam_ref, lam_x_ref, out_ref):
    shift = lam_x_ref[pl.ds(lax.axis_index("space"), 1), :]
    sub = iota((8, 128), 0)
    total = jnp.zeros((64, 88), jnp.float32)
    for r in range(0, ROWS, 2):
        left, right = [], []
        for row in (r, r + 1):
            b = all_ref[pl.ds(row, SLICES, stride=2 * ROWS), :]
            d = all_ref[pl.ds(ROWS + row, SLICES, stride=2 * ROWS), :]
            lam = lam_ref[row : row + 1, :] + shift
            lam2 = lam * lam
            lam4 = lam2 * lam2
            lam3 = lam2 * lam
            first = d[0:1] + lam * b[0:1]
            powers = jnp.where(sub == 0, 1.0, jnp.where(sub == 1, lam, jnp.where(sub == 2, lam2, lam3)))
            b4 = b * lam4
            b8 = b4 * lam4
            left.append(jnp.concatenate([b, b4, b8, b8 * lam4], axis=0))
            right.append(
                jnp.concatenate([d, d * lam, d * lam2, d * lam3, b, powers * first], axis=0)
            )
        total = total + dot(
            jnp.concatenate(left, axis=1), jnp.concatenate(right, axis=1), ((1,), (1,))
        )
    total = jnp.concatenate([total, jnp.zeros((64, 40), jnp.float32)], axis=1)
    a = [total[16 * i : 16 * i + 16] for i in range(4)]
    lane = iota((16, 128), 1)
    low = jnp.where(lane < 64, a[0], pltpu.roll(a[1], 64, 1))
    high = jnp.where(lane < 64, a[2], pltpu.roll(a[3], 64, 1))
    high = jnp.where((lane >= 96) & (lane < 112), pltpu.roll(a[0], 32, 1), high)
    for i in range(4):
        at = 112 + 4 * i
        high = jnp.where((lane >= at) & (lane < at + 4), pltpu.roll(a[i], (at - 80) % 128, 1), high)
    out_ref[:, :128] = low
    out_ref[:, 128:] = high


def solve_kernel(sums_ref, all_ref, inv_z_ref, lam_ref, lam_x_ref, out_ref):
    shift = lam_x_ref[pl.ds(lax.axis_index("space"), 1), :]
    slice_index = lax.axis_index("tm")
    parts = sums_ref.shape[0]
    total = sums_ref[0]
    for i in range(1, parts):
        total = total + sums_ref[i]
    low, high = total[:, :128], total[:, 128:]
    lane = iota((16, 128), 1)
    sub = iota((16, 128), 0)
    columns = [jnp.broadcast_to(high[:, 96 + i : 97 + i], (16, 128)) for i in range(SLICES)]
    for i in range(SLICES):
        column = columns[i]
        factor = jnp.where(sub == i, column - 1.0, column) * (1.0 / column[i : i + 1])
        for j in range(i + 1, SLICES):
            columns[j] = columns[j] - factor * columns[j][i : i + 1]
        low, high = low - factor * low[i : i + 1], high - factor * high[i : i + 1]

    def shifted(pair, by):
        rolled = [pltpu.roll(v, 128 - by, 1) for v in pair]
        inside = lane < 128 - by
        return jnp.where(inside, rolled[0], rolled[1]), jnp.where(inside, rolled[1], 0.0)

    diag = (lane & 15) == sub
    spread = (lane >> 3) == sub
    block = (iota((8, 128), 1) & 7) == iota((8, 128), 0)
    starts = [high, None]
    one = (low, jnp.where(lane < 96, high, 0.0))
    one_next = shifted(one, 16)
    twice = dot(low[:, :16], jnp.concatenate([low, high], axis=1))
    starts[1] = twice[:, 128:] + pltpu.roll(high, 127, 1)
    two = (twice[:, :128] + one_next[0], jnp.where(lane < 80, twice[:, 128:] + one_next[1], 0.0))
    two_next = shifted(two, 16)
    acc_one = acc_two = None
    first = jnp.where(iota((1, 128), 1) < 8, 1.0, 0.0)
    weights = [jnp.where(block, first, 0.0)]
    for n in range(0, SLICES, 2):
        found = []
        for acc, start in ((acc_one, starts[0]), (acc_two, starts[1])):
            if n == SLICES - 2 and found:
                break
            at = jnp.where(lane == 112 + n, start, 0.0)
            if n > 0:
                at = at + jnp.where(lane < 16, acc[0], 0.0)
            c = jnp.sum(at, axis=1, keepdims=True)
            found.append(c)
            weights.append(
                jnp.where(block, jnp.sum(jnp.where(spread, c, 0.0), axis=0, keepdims=True), 0.0)
            )
        if n < SLICES - 2:
            older, newer = [
                jnp.sum(jnp.where(diag, c, 0.0), axis=0, keepdims=True) for c in found
            ]
            grown_one = [a * newer + b * older for a, b in zip(one, one_next)]
            grown_two = [a * newer + b * older for a, b in zip(two, two_next)]
            if n > 0:
                grown_one = [a + b for a, b in zip(grown_one, shifted(acc_one, 32))]
                grown_two = [a + b for a, b in zip(grown_two, shifted(acc_two, 32))]
            acc_one, acc_two = grown_one, grown_two
    weights = jnp.concatenate(weights, axis=0)
    tiles = []
    for g in range(3):
        rows = slice(8 * g, 8 * g + 8)
        lam = lam_ref[rows] + shift
        d = all_ref[:, ROWS + 8 * g : ROWS + 8 * g + 8, :].reshape(128, 128)
        terms = dot(weights, d)
        b0 = all_ref[0, rows, :]
        value = terms[0:8] + lam * b0
        for k in range(1, SLICES):
            value = jnp.where(k <= slice_index, lam * value + terms[8 * k : 8 * k + 8], value)
        b_n = all_ref[slice_index, rows, :]
        d_n = all_ref[slice_index, ROWS + 8 * g : ROWS + 8 * g + 8, :]
        tiles.append(value - d_n - lam * b_n)
    group = iota((8, 128), 1) // 32
    rest = jnp.zeros((8, 128), jnp.float32)
    for c in range(3):
        rest = jnp.where(group == c, pltpu.roll(tiles[c], (32 * c - 96) % 128, 1), rest)
    planes = dot_halves(inv_z_ref[...], jnp.concatenate(tiles + [rest], axis=0))
    for s in range(DEVICES_Z):
        out_ref[s] = planes[2 * s : 2 * s + 2]


def pair_kernel(mine_ref, other_ref, out_ref):
    total = mine_ref[...] + other_ref[...]
    for i in range(out_ref.shape[0]):
        out_ref[i] = total


def finish_kernel(fine_ref, modes_ref, inv_x_ref, inv_y_ref, out_hbm, out_ref, sem):
    copies = []
    for q in range(2):
        both = dot_halves(dot_halves(inv_x_ref[...], modes_ref[:, q, :]), inv_y_ref[...])
        for c in range(3):
            carried = both[:, c * CY : (c + 1) * CY]
            for k in range(COARSEN):
                z = COARSEN * q + k
                out_ref[c, z] = fine_ref[c, z] + carried
            planes = pl.ds(COARSEN * q, COARSEN)
            copy = pltpu.make_async_copy(
                out_ref.at[c, planes], out_hbm.at[c, planes], sem.at[q, c]
            )
            copy.start()
            copies.append(copy)
    for copy in copies:
        copy.wait()


VMEM = pl.BlockSpec(memory_space=pltpu.VMEM)
SMEM = pl.BlockSpec(memory_space=pltpu.SMEM)
HBM = pl.BlockSpec(memory_space=pltpu.HBM)


def fast(x):
    return pltpu.with_memory_space_constraint(x, pltpu.VMEM)


def call(kernel, outs, specs, scratch=(), out_specs=None):
    return pl.pallas_call(
        kernel,
        out_shape=outs,
        in_specs=specs,
        out_specs=VMEM if out_specs is None else out_specs,
        scratch_shapes=list(scratch),
    )


def near_array(*shape):
    return pltpu.VMEM(shape, jnp.float32)


def far_array(*shape):
    return jax.ShapeDtypeStruct(shape, jnp.float32)


def local(starts, strain):
    first = ("fwd_x", "wide_fwd_y")
    con = {k: v if k in first else fast(jnp.asarray(v)) for k, v in constants().items()}
    field, rates = starts[0], strain[0]
    count = lax.axis_size("space")

    coarse = call(
        coarse_kernel,
        near_array(NX, 8, 128),
        [HBM] * 4,
        [
            pltpu.VMEM(field.shape, jnp.float32),
            pltpu.VMEM(rates.shape, jnp.bfloat16),
            pltpu.VMEM((NX, NX), jnp.float32),
            pltpu.VMEM((3 * CY, 128), jnp.float32),
            pltpu.VMEM((6, 3, CX, CY), jnp.float32),
            pltpu.SemaphoreType.DMA((3, 2)),
        ],
    )(field, rates, con["fwd_x"], con["wide_fwd_y"])
    coarse = lax.all_to_all(coarse, "space", 0, 0, tiled=True)
    mine = call(depth_kernel, near_array(SLICES, 2 * ROWS, 128), [VMEM] * 4)(
        fast(coarse.reshape(128, 128)), con["fwd_z"], con["lam_full"], con["lam_x"]
    )
    later, mine = lax.optimization_barrier((field, mine))
    every = lax.all_to_all(mine, "tm", 0, 0, tiled=True)
    below = lax.ppermute(later[:, DEPTH - 2 :], "space", [(i, i + 1) for i in range(count - 1)])
    above = lax.ppermute(later[:, :2], "space", [(i + 1, i) for i in range(count - 1)])
    share = call(gram_kernel, near_array(SLICES, 256), [VMEM] * 3)(
        fast(every.reshape(SLICES * 2 * ROWS, 128)), con["lam"], con["lam_x"]
    )
    fine = call(fine_kernel, near_array(*field.shape), [VMEM] * 4)(
        later, rates, fast(below), fast(above)
    )
    other = lax.ppermute(share, "space", [(i, i ^ 1) for i in range(count)])
    pair = call(pair_kernel, near_array(count // 2, *share.shape), [VMEM] * 2)(
        fast(share), fast(other)
    )
    groups = [list(range(0, count, 2)), list(range(1, count, 2))]
    shares = lax.all_to_all(pair, "space", 0, 0, axis_index_groups=groups, tiled=True)
    carried = call(solve_kernel, near_array(DEVICES_Z, 2, 128), [VMEM] * 5)(
        fast(shares), fast(every), con["inv_z"], con["lam"], con["lam_x"]
    )
    carried = lax.all_to_all(carried, "space", 0, 0, tiled=True)
    corrected = call(
        finish_kernel,
        far_array(*field.shape),
        [VMEM] * 4,
        [pltpu.VMEM(field.shape, jnp.float32), pltpu.SemaphoreType.DMA((2, 3))],
        HBM,
    )(fast(fine), fast(carried), con["inv_x"], con["wide_inv_y"])
    return corrected[None]


def solution(mesh):
    return jax.shard_map(
        local,
        mesh=mesh,
        in_specs=(P("tm", None, "space", None, None), P("tm", None, "space", None, None)),
        out_specs=P("tm", None, "space", None, None),
        check_vma=False,
    )
```

```python
import functools

import jax
import jax.numpy as jnp
import numpy as np
from jax import lax
from jax.experimental import pallas as pl
from jax.experimental.pallas import tpu as pltpu
from jax.sharding import PartitionSpec as P

COARSEN = 4
SLICES = 16
DEVICES_Z = 16
NX, NY, NZ = 16, 32, 32
CX, CY = 64, 128
DEPTH = 8

kernel_near = 0.8
kernel_far = 0.2
diffusion = 0.08
coarse_rate = 0.1

ROWS = 24
HIGH = lax.Precision.HIGHEST


def real_fourier(n):
    x = np.arange(n)
    rows, freq = [np.full(n, 1.0 / np.sqrt(n))], [0]
    for k in range(1, n // 2):
        rows.append(np.sqrt(2.0 / n) * np.cos(2 * np.pi * k * x / n))
        rows.append(np.sqrt(2.0 / n) * np.sin(2 * np.pi * k * x / n))
        freq += [k, k]
    rows.append(((-1.0) ** x) / np.sqrt(n))
    freq.append(n // 2)
    return np.stack(rows), 2 * np.cos(2 * np.pi * np.array(freq) / n)


def constants():
    fx, ex = real_fourier(NX)
    fy, ey = real_fourier(NY)
    k = np.arange(1, NZ + 1)
    sz = np.sqrt(2.0 / (NZ + 1)) * np.sin(np.pi * np.outer(k, k) / (NZ + 1))
    ez = 2 * np.cos(np.pi * k / (NZ + 1))
    spread_x = np.repeat(np.eye(NX), COARSEN, axis=0)
    spread_y = np.repeat(np.eye(NY), COARSEN, axis=0)
    fwd_x = fx / 16.0
    fwd_y = spread_y @ fy.T / 4.0
    inv_x = spread_x @ fx.T
    inv_y = fy @ spread_y.T
    wide_fwd_y = np.zeros((3 * CY, 128))
    wide_inv_y = np.zeros((128, 3 * CY))
    for c in range(3):
        wide_fwd_y[c * CY : (c + 1) * CY, 32 * c : 32 * c + 32] = fwd_y
        wide_inv_y[32 * c : 32 * c + 32, c * CY : (c + 1) * CY] = inv_y
    fwd_z = np.zeros((2 * NZ, DEVICES_Z, 8))
    for s in range(DEVICES_Z):
        for q in range(2):
            fwd_z[:NZ, s, q] = sz[:, 2 * s + q]
            fwd_z[NZ:, s, 2 + q] = sz[:, 2 * s + q]
        if s > 0:
            fwd_z[NZ:, s, 4] = sz[:, 2 * s - 1]
        if s < DEVICES_Z - 1:
            fwd_z[NZ:, s, 5] = sz[:, 2 * s + 2]
    full = 1.0 + coarse_rate * (ez[:, None] + ey[None, :] - 6.0)
    packed = np.zeros((ROWS, 128))
    for c in range(3):
        packed[:, 32 * c : 32 * c + 32] = full[:ROWS]
        packed[8 * c : 8 * c + 8, 96:] = full[ROWS:]
    f = lambda a: np.asarray(a, np.float32)
    return dict(
        fwd_x=f(fwd_x),
        wide_fwd_y=f(wide_fwd_y),
        inv_x=f(inv_x),
        wide_inv_y=f(wide_inv_y),
        fwd_z=f(fwd_z.reshape(2 * NZ, DEVICES_Z * 8)),
        inv_z=f(sz),
        lam=f(packed),
        lam_full=f(np.tile(full, (1, 4))),
        lam_x=f(np.tile(coarse_rate * ex[:, None], (1, 128))),
    )


def dot(a, b, dims=((1,), (0,))):
    return lax.dot_general(
        a, b, (dims, ((), ())), precision=HIGH, preferred_element_type=jnp.float32
    )


def iota(shape, dim):
    return lax.broadcasted_iota(jnp.int32, shape, dim)


def around(f, width):
    total = pltpu.roll(f, width, 0) + pltpu.roll(f, CX - width, 0)
    return total + pltpu.roll(f, width, 1) + pltpu.roll(f, CY - width, 1)


def coarse_kernel(
    field_hbm, strain_hbm, fwd_x_hbm, fwd_y_hbm, coarse_ref,
    field_ref, strain_ref, fwd_x_ref, fwd_y_ref, sums, sem,
):
    near = diffusion * kernel_near
    far = diffusion * kernel_far

    def arrays(q):
        planes = pl.ds(COARSEN * q, COARSEN)
        return [
            pltpu.make_async_copy(field_hbm.at[:, planes], field_ref.at[:, planes], sem.at[q, 0]),
            pltpu.make_async_copy(strain_hbm.at[:, planes], strain_ref.at[:, planes], sem.at[q, 1]),
        ]

    tables = [
        pltpu.make_async_copy(fwd_x_hbm, fwd_x_ref, sem.at[2, 0]),
        pltpu.make_async_copy(fwd_y_hbm, fwd_y_ref, sem.at[2, 1]),
    ]
    for copy in arrays(0) + arrays(1) + tables:
        copy.start()

    def block(q, _):
        for copy in arrays(q):
            copy.wait()
        basis = [None] * 3
        stretch = [None] * 3
        for k in range(COARSEN):
            z = COARSEN * q + k
            comps = [field_ref[c, z] for c in range(3)]
            for c in range(3):
                acc = strain_ref[3 * c, z].astype(jnp.float32) * comps[0]
                for j in range(1, 3):
                    acc = acc + strain_ref[3 * c + j, z].astype(jnp.float32) * comps[j]
                stretch[c] = acc if k == 0 else stretch[c] + acc
                basis[c] = comps[c] if k == 0 else basis[c] + comps[c]
        for c in range(3):
            total = basis[c]
            sums[q, c] = total
            sums[2 + q, c] = (
                (1.0 - 4.0 * (near + far)) * total
                + stretch[c]
                + near * around(total, 1)
                + far * around(total, 2)
            )
        return 0

    lax.fori_loop(0, 2, block, 0)
    for c in range(3):
        low = [diffusion * field_ref[c, 4 * q] + far * field_ref[c, 4 * q + 1] for q in range(2)]
        high = [diffusion * field_ref[c, 4 * q + 3] + far * field_ref[c, 4 * q + 2] for q in range(2)]
        middle = low[1] - high[0]
        sums[2, c] += middle - low[0]
        sums[3, c] -= middle + high[1]
        sums[4, c] = low[0]
        sums[5, c] = high[1]
    for copy in tables:
        copy.wait()
    along_x = []
    for q in range(6):
        wide = []
        for c in range(3):
            rows = [sums[q, c, pl.ds(k, NX, stride=COARSEN), :] for k in range(COARSEN)]
            wide.append((rows[0] + rows[1]) + (rows[2] + rows[3]))
        along_x.append(dot(fwd_x_ref[...], jnp.concatenate(wide, axis=1)))
    modes = dot(jnp.concatenate(along_x, axis=0), fwd_y_ref[...])
    for q in range(6):
        coarse_ref[:, q, :] = modes[NX * q : NX * (q + 1)]
    for q in range(6, 8):
        coarse_ref[:, q, :] = jnp.zeros((NX, 128), jnp.float32)


def fine_kernel(field_ref, strain_ref, below_ref, above_ref, fine_ref):
    near = diffusion * kernel_near
    far = diffusion * kernel_far
    centre = 1.0 - 6.0 * (near + far)

    def plane(z, _):
        up1, up2 = jnp.minimum(z + 1, DEPTH - 1), jnp.minimum(z + 2, DEPTH - 1)
        dn1, dn2 = jnp.maximum(z - 1, 0), jnp.maximum(z - 2, 0)
        w_up1 = jnp.where(z + 1 < DEPTH, near, 0.0).astype(jnp.float32)
        w_up2 = jnp.where(z + 2 < DEPTH, far, 0.0).astype(jnp.float32)
        w_dn1 = jnp.where(z >= 1, near, 0.0).astype(jnp.float32)
        w_dn2 = jnp.where(z >= 2, far, 0.0).astype(jnp.float32)
        comps = [field_ref[c, z] for c in range(3)]
        for c in range(3):
            f = comps[c]
            acc = centre * f + near * around(f, 1) + far * around(f, 2)
            acc = acc + w_up1 * field_ref[c, up1] + w_dn1 * field_ref[c, dn1]
            acc = acc + w_up2 * field_ref[c, up2] + w_dn2 * field_ref[c, dn2]
            for j in range(3):
                acc = acc + strain_ref[3 * c + j, z].astype(jnp.float32) * comps[j]
            fine_ref[c, z] = acc
        return 0

    lax.fori_loop(0, DEPTH, plane, 0)
    for c in range(3):
        fine_ref[c, 0] += near * below_ref[c, 1] + far * below_ref[c, 0]
        fine_ref[c, 1] += far * below_ref[c, 1]
        fine_ref[c, DEPTH - 2] += far * above_ref[c, 0]
        fine_ref[c, DEPTH - 1] += near * above_ref[c, 0] + far * above_ref[c, 1]


def depth_kernel(modes_ref, fwd_z_ref, lam_ref, lam_x_ref, out_ref):
    lam = lam_ref[...] + lam_x_ref[pl.ds(lax.axis_index("space"), 1), :]
    both = dot(fwd_z_ref[...], modes_ref[...])
    basis = both[:NZ]
    defect = both[NZ:] - lam * basis
    group = iota((8, 128), 1) // 32
    tiles = []
    for v in (basis, defect):
        rest = v[ROWS:]
        for c in range(3):
            moved = pltpu.roll(rest, 96 - 32 * c, 1)
            tiles.append(jnp.where(group == 3, moved, v[8 * c : 8 * c + 8]))
    packed = jnp.concatenate(tiles, axis=0)
    for m in range(SLICES):
        out_ref[m] = packed


def gram_kernel(all_ref, lam_ref, lam_x_ref, out_ref):
    shift = lam_x_ref[pl.ds(lax.axis_index("space"), 1), :]
    sub = iota((8, 128), 0)
    total = jnp.zeros((64, 88), jnp.float32)
    for r in range(0, ROWS, 2):
        left, right = [], []
        for row in (r, r + 1):
            b = all_ref[pl.ds(row, SLICES, stride=2 * ROWS), :]
            d = all_ref[pl.ds(ROWS + row, SLICES, stride=2 * ROWS), :]
            lam = lam_ref[row : row + 1, :] + shift
            lam2 = lam * lam
            lam4 = lam2 * lam2
            lam3 = lam2 * lam
            first = d[0:1] + lam * b[0:1]
            powers = jnp.where(sub == 0, 1.0, jnp.where(sub == 1, lam, jnp.where(sub == 2, lam2, lam3)))
            b4 = b * lam4
            b8 = b4 * lam4
            left.append(jnp.concatenate([b, b4, b8, b8 * lam4], axis=0))
            right.append(
                jnp.concatenate([d, d * lam, d * lam2, d * lam3, b, powers * first], axis=0)
            )
        total = total + dot(
            jnp.concatenate(left, axis=1), jnp.concatenate(right, axis=1), ((1,), (1,))
        )
    total = jnp.concatenate([total, jnp.zeros((64, 40), jnp.float32)], axis=1)
    a = [total[16 * i : 16 * i + 16] for i in range(4)]
    lane = iota((16, 128), 1)
    low = jnp.where(lane < 64, a[0], pltpu.roll(a[1], 64, 1))
    high = jnp.where(lane < 64, a[2], pltpu.roll(a[3], 64, 1))
    high = jnp.where((lane >= 96) & (lane < 112), pltpu.roll(a[0], 32, 1), high)
    for i in range(4):
        at = 112 + 4 * i
        high = jnp.where((lane >= at) & (lane < at + 4), pltpu.roll(a[i], (at - 80) % 128, 1), high)
    out_ref[:, :128] = low
    out_ref[:, 128:] = high


def solve_kernel(sums_ref, all_ref, inv_z_ref, lam_ref, lam_x_ref, out_ref):
    shift = lam_x_ref[pl.ds(lax.axis_index("space"), 1), :]
    slice_index = lax.axis_index("tm")
    parts = sums_ref.shape[0]
    total = sums_ref[0]
    for i in range(1, parts):
        total = total + sums_ref[i]
    low, high = total[:, :128], total[:, 128:]
    lane = iota((16, 128), 1)
    sub = iota((16, 128), 0)
    columns = [jnp.broadcast_to(high[:, 96 + i : 97 + i], (16, 128)) for i in range(SLICES)]
    for i in range(SLICES):
        column = columns[i]
        factor = jnp.where(sub == i, column - 1.0, column) * (1.0 / column[i : i + 1])
        for j in range(i + 1, SLICES):
            columns[j] = columns[j] - factor * columns[j][i : i + 1]
        low, high = low - factor * low[i : i + 1], high - factor * high[i : i + 1]

    def shifted(pair, by):
        rolled = [pltpu.roll(v, 128 - by, 1) for v in pair]
        inside = lane < 128 - by
        return jnp.where(inside, rolled[0], rolled[1]), jnp.where(inside, rolled[1], 0.0)

    diag = (lane & 15) == sub
    spread = (lane >> 3) == sub
    block = (iota((8, 128), 1) & 7) == iota((8, 128), 0)
    starts = [high, None]
    one = (low, jnp.where(lane < 96, high, 0.0))
    one_next = shifted(one, 16)
    twice = dot(low[:, :16], jnp.concatenate([low, high], axis=1))
    starts[1] = twice[:, 128:] + pltpu.roll(high, 127, 1)
    two = (twice[:, :128] + one_next[0], jnp.where(lane < 80, twice[:, 128:] + one_next[1], 0.0))
    two_next = shifted(two, 16)
    acc_one = acc_two = None
    first = jnp.where(iota((1, 128), 1) < 8, 1.0, 0.0)
    weights = [jnp.where(block, first, 0.0)]
    for n in range(0, SLICES, 2):
        found = []
        for acc, start in ((acc_one, starts[0]), (acc_two, starts[1])):
            if n == SLICES - 2 and found:
                break
            at = jnp.where(lane == 112 + n, start, 0.0)
            if n > 0:
                at = at + jnp.where(lane < 16, acc[0], 0.0)
            c = jnp.sum(at, axis=1, keepdims=True)
            found.append(c)
            weights.append(
                jnp.where(block, jnp.sum(jnp.where(spread, c, 0.0), axis=0, keepdims=True), 0.0)
            )
        if n < SLICES - 2:
            older, newer = [
                jnp.sum(jnp.where(diag, c, 0.0), axis=0, keepdims=True) for c in found
            ]
            grown_one = [a * newer + b * older for a, b in zip(one, one_next)]
            grown_two = [a * newer + b * older for a, b in zip(two, two_next)]
            if n > 0:
                grown_one = [a + b for a, b in zip(grown_one, shifted(acc_one, 32))]
                grown_two = [a + b for a, b in zip(grown_two, shifted(acc_two, 32))]
            acc_one, acc_two = grown_one, grown_two
    weights = jnp.concatenate(weights, axis=0)
    tiles = []
    defects = [all_ref[:, ROWS + 8 * g : ROWS + 8 * g + 8, :].reshape(128, 128) for g in range(3)]
    every_term = dot(weights, jnp.concatenate(defects, axis=1))
    for g in range(3):
        rows = slice(8 * g, 8 * g + 8)
        lam = lam_ref[rows] + shift
        terms = every_term[:, 128 * g : 128 * g + 128]
        b0 = all_ref[0, rows, :]
        value = terms[0:8] + lam * b0
        for k in range(1, SLICES):
            value = jnp.where(k <= slice_index, lam * value + terms[8 * k : 8 * k + 8], value)
        b_n = all_ref[slice_index, rows, :]
        d_n = all_ref[slice_index, ROWS + 8 * g : ROWS + 8 * g + 8, :]
        tiles.append(value - d_n - lam * b_n)
    group = iota((8, 128), 1) // 32
    rest = jnp.zeros((8, 128), jnp.float32)
    for c in range(3):
        rest = jnp.where(group == c, pltpu.roll(tiles[c], (32 * c - 96) % 128, 1), rest)
    planes = dot(inv_z_ref[...], jnp.concatenate(tiles + [rest], axis=0))
    for s in range(DEVICES_Z):
        out_ref[s] = planes[2 * s : 2 * s + 2]


def pair_kernel(mine_ref, other_ref, out_ref):
    total = mine_ref[...] + other_ref[...]
    for i in range(out_ref.shape[0]):
        out_ref[i] = total


def finish_kernel(fine_ref, modes_ref, inv_x_ref, inv_y_ref, out_hbm, out_ref, sem):
    copies = []
    wide = dot(inv_x_ref[...], jnp.concatenate([modes_ref[:, q, :] for q in range(2)], axis=1))
    tall = jnp.concatenate([wide[:, :128], wide[:, 128:]], axis=0)
    blocks = dot(tall, inv_y_ref[...])
    for q in range(2):
        both = blocks[CX * q : CX * q + CX]
        for c in range(3):
            carried = both[:, c * CY : (c + 1) * CY]
            for k in range(COARSEN):
                z = COARSEN * q + k
                out_ref[c, z] = fine_ref[c, z] + carried
            planes = pl.ds(COARSEN * q, COARSEN)
            copy = pltpu.make_async_copy(
                out_ref.at[c, planes], out_hbm.at[c, planes], sem.at[q, c]
            )
            copy.start()
            copies.append(copy)
    for copy in copies:
        copy.wait()


VMEM = pl.BlockSpec(memory_space=pltpu.VMEM)
SMEM = pl.BlockSpec(memory_space=pltpu.SMEM)
HBM = pl.BlockSpec(memory_space=pltpu.HBM)


def fast(x):
    return pltpu.with_memory_space_constraint(x, pltpu.VMEM)


def call(kernel, outs, specs, scratch=(), out_specs=None):
    return pl.pallas_call(
        kernel,
        out_shape=outs,
        in_specs=specs,
        out_specs=VMEM if out_specs is None else out_specs,
        scratch_shapes=list(scratch),
    )


def near_array(*shape):
    return pltpu.VMEM(shape, jnp.float32)


def far_array(*shape):
    return jax.ShapeDtypeStruct(shape, jnp.float32)


def local(starts, strain):
    first = ("fwd_x", "wide_fwd_y")
    con = {k: v if k in first else fast(jnp.asarray(v)) for k, v in constants().items()}
    field, rates = starts[0], strain[0]
    count = lax.axis_size("space")

    coarse = call(
        coarse_kernel,
        near_array(NX, 8, 128),
        [HBM] * 4,
        [
            pltpu.VMEM(field.shape, jnp.float32),
            pltpu.VMEM(rates.shape, jnp.bfloat16),
            pltpu.VMEM((NX, NX), jnp.float32),
            pltpu.VMEM((3 * CY, 128), jnp.float32),
            pltpu.VMEM((6, 3, CX, CY), jnp.float32),
            pltpu.SemaphoreType.DMA((3, 2)),
        ],
    )(field, rates, con["fwd_x"], con["wide_fwd_y"])
    coarse = lax.all_to_all(coarse, "space", 0, 0, tiled=True)
    mine = call(depth_kernel, near_array(SLICES, 2 * ROWS, 128), [VMEM] * 4)(
        fast(coarse.reshape(128, 128)), con["fwd_z"], con["lam_full"], con["lam_x"]
    )
    later, mine = lax.optimization_barrier((field, mine))
    every = lax.all_to_all(mine, "tm", 0, 0, tiled=True)
    below = lax.ppermute(later[:, DEPTH - 2 :], "space", [(i, i + 1) for i in range(count - 1)])
    above = lax.ppermute(later[:, :2], "space", [(i + 1, i) for i in range(count - 1)])
    share = call(gram_kernel, near_array(SLICES, 256), [VMEM] * 3)(
        fast(every.reshape(SLICES * 2 * ROWS, 128)), con["lam"], con["lam_x"]
    )
    fine = call(fine_kernel, near_array(*field.shape), [VMEM] * 4)(
        later, rates, fast(below), fast(above)
    )
    other = lax.ppermute(share, "space", [(i, i ^ 1) for i in range(count)])
    pair = call(pair_kernel, near_array(count // 2, *share.shape), [VMEM] * 2)(
        fast(share), fast(other)
    )
    groups = [list(range(0, count, 2)), list(range(1, count, 2))]
    shares = lax.all_to_all(pair, "space", 0, 0, axis_index_groups=groups, tiled=True)
    carried = call(solve_kernel, near_array(DEVICES_Z, 2, 128), [VMEM] * 5)(
        fast(shares), fast(every), con["inv_z"], con["lam"], con["lam_x"]
    )
    carried = lax.all_to_all(carried, "space", 0, 0, tiled=True)
    corrected = call(
        finish_kernel,
        far_array(*field.shape),
        [VMEM] * 4,
        [pltpu.VMEM(field.shape, jnp.float32), pltpu.SemaphoreType.DMA((2, 3))],
        HBM,
    )(fast(fine), fast(carried), con["inv_x"], con["wide_inv_y"])
    return corrected[None]


def solution(mesh):
    return jax.shard_map(
        local,
        mesh=mesh,
        in_specs=(P("tm", None, "space", None, None), P("tm", None, "space", None, None)),
        out_specs=P("tm", None, "space", None, None),
        check_vma=False,
    )
```
